512 devices in a mesh: attn: 32 (over z, core), egrp: 4 (over x), eslice: 4 (over y).
Axes of the slice: x: 4, y: 4, z: 16, core: 2. Of those that a mesh axis runs over, the one named last changes fastest.
Arguments:
- queries: bfloat16 [384, 3072], P(('attn', 'eslice'), 'egrp'), may hold values from -20 to 20
- new_key: bfloat16 [384, 512], P(('attn', 'eslice'), 'egrp'), may hold values from -5 to 5
- new_value: bfloat16 [384, 512], P(('attn', 'eslice'), 'egrp'), may hold values from -5 to 5
- cache_keys: bfloat16 [384, 512, 512], P(('attn', 'eslice'), None, 'egrp'), may hold values from -20 to 20
- cache_values: bfloat16 [384, 512, 512], P(('attn', 'eslice'), None, 'egrp'), may hold values from -5 to 5
- lengths: int32 [384], P(('attn', 'eslice')), may hold values from 2 to 512, as said below
- out_proj: bfloat16 [4, 768, 6144], P('egrp', 'attn', 'eslice'), may hold values from -0.21875 to 0.21875
- residual: bfloat16 [384, 6144], P('attn', 'eslice'), may hold values from -24 to 24
- norm_gain: bfloat16 [6144], P('eslice'), may hold values from 0.25 to 1.75
- expert_ids: int32 [384, 4], P('attn'), may hold values from 0 to 7, all different within a row; in each aligned block of 384 rows (0 to 383, 384 to 767, ...) at most 288 rows name the same one
- gate_weights: bfloat16 [384, 4], P('attn'), may hold values from 0.099609375 to 1
- gate_proj: bfloat16 [8, 5376, 6144], P('egrp', 'attn', 'eslice'), may hold values from -0.078125 to 0.078125
- up_proj: bfloat16 [8, 5376, 6144], P('egrp', 'attn', 'eslice'), may hold values from -0.078125 to 0.078125
- down_proj: bfloat16 [8, 5376, 6144], P('egrp', 'attn', 'eslice'), may hold values from -0.15625 to 0.15625
Outputs:
- layer_out: bfloat16 [384, 6144], P(('attn', 'egrp'), 'eslice')
The draws below stay inside these ranges and needn't reach their ends.
Inputs may be any that keep to these rules, and one draw needn't show every extreme that they name: `lengths`: some request has all 512 slots live. `expert_ids`: each request names 4 different experts; no expert is named by more than 288 requests, a bound that some block reaches.
All inputs are finite; a program needn't handle non-finite values.
Results may differ from the reference program's by a relative error of at most 0.02.
Values may be sent and summed in bfloat16 or wider, within the bound.
A program may use at most 64 MiB of HBM per device.

```python
import math
import jax
import jax.numpy as jnp
import numpy as np
from jax import lax

D = 6144
HQ = 24
KVH = 4
HD = 128
E = 8
TOPK = 4
FF = 5376
L = 512
REQ = 384
CAP = 288


def draw_queries(key, part):
    key = jax.random.fold_in(key, 1)
    fresh = jnp.clip(jax.random.normal(key, (REQ, KVH, HQ // KVH, HD), jnp.float32), -5.0, 5.0)
    return fresh.reshape(REQ, HQ * HD).astype(jnp.bfloat16)


def draw_cache_keys(key, part):
    key = jax.random.fold_in(key, 2)
    fresh = jnp.clip(jax.random.normal(key, (REQ, L, KVH, HD), jnp.float32), -5.0, 5.0)
    return fresh.reshape(REQ, L, KVH * HD).astype(jnp.bfloat16)


def draw_lengths(key, part):
    key = jax.random.fold_in(key, 3)
    drawn = jax.random.randint(jax.random.fold_in(key, 1), (REQ,), 2, L + 1)
    longest = jax.random.randint(jax.random.fold_in(key, 2), (), 0, REQ)
    return drawn.at[longest].set(L).astype(jnp.int32)


def draw_residual(key, part):
    key = jax.random.fold_in(key, 5)
    ramp = jnp.arange(D, dtype=jnp.float32) / D
    jitter = jax.random.uniform(jax.random.fold_in(key, 1), (D,), jnp.float32)
    column_scale = 0.3 * 10.0 ** (0.6 * ramp + 0.4 * jitter)
    fresh = jnp.clip(jax.random.normal(jax.random.fold_in(key, 2), (REQ, D), jnp.float32), -4.0, 4.0)
    return (fresh * column_scale[None, :]).astype(jnp.bfloat16)


def steps_of(own_key, extent, shards, smallest, top_value):
    loudness = 1.0
    for position, parts in shards:
        draws = jax.random.uniform(jax.random.fold_in(jax.random.fold_in(own_key, 6), position), (parts,), jnp.float32, smallest / len(shards), top_value / len(shards))
        loudness = loudness * jnp.repeat(jnp.exp(draws), extent[position] // parts).reshape((-1,) + (1,) * (len(extent) - 1 - position))
    return loudness


def deal_out(key, own, number, rows, number_of, top, limit, lean):
    order = jax.random.permutation(key, number_of)
    packed, usual = portions_of(number_of, rows * top, limit, lean, True), portions_of(number_of, rows * top, limit, lean, False)
    places = jnp.arange(number_of)

    def named(sizes, offset_by):
        used = int((sizes > 0).sum())
        fixed = max(1, used // 4)
        passed = fixed + (places - fixed + offset_by * (used - fixed)) % max(1, number_of - fixed)
        return jnp.zeros((number_of,), jnp.int32).at[order[jnp.where(places < fixed, places, passed)]].set(jnp.asarray(sizes, jnp.int32))

    sizes = jnp.where(number % 4 == 0, named(packed, number // 4), named(usual, number - number // 4 - 1))
    mixed = jax.random.permutation(jax.random.fold_in(own, 3), number_of)
    source_of, sink = mixed[0:number_of // 2 * 2:2], mixed[1:number_of // 2 * 2:2]
    margin = jnp.minimum(sizes[source_of] - 1, limit - sizes[sink]) // 2
    margin = jnp.where((source_of == order[0]) | (sink == order[0]) | (sizes[sink] == 0), 0, jnp.maximum(margin, 0))
    passed = jax.random.randint(jax.random.fold_in(own, 4), (number_of // 2,), 0, 1 << 20) % (margin + 1)
    sizes = sizes.at[source_of].add(-passed).at[sink].add(passed)
    members = jnp.searchsorted(jnp.cumsum(sizes), jnp.arange(rows * top), side="right").astype(jnp.int32)
    listing = members.reshape(top, rows).T
    listing = listing[jax.random.permutation(jax.random.fold_in(own, 1), rows)]
    offset_by = jax.random.randint(jax.random.fold_in(own, 2), (rows, 1), 0, top)
    return jnp.take_along_axis(listing, (jnp.arange(top)[None, :] + offset_by) % top, axis=1)


def portions_of(number_of, total, most, slope, full):
    weights = [(1 << 20) // math.isqrt(rank ** slope) + 1 for rank in range(1, number_of + 1)]
    largest = most if full else min(most, max(-(-total // number_of), total * weights[0] // sum(weights)))
    least = 1 if total - largest >= number_of - 1 else 0
    counts, spare = [largest] + [least] * (number_of - 1), total - largest - least * (number_of - 1)
    while spare > 0:
        candidates = [i for i in range(1, number_of) if counts[i] < largest] or [i for i in range(1, number_of) if counts[i] < most]
        mass, remaining = sum([weights[i] for i in candidates]), spare
        for i in candidates:
            addition = min(most - counts[i], max(1, remaining * weights[i] // mass), spare)
            counts[i] = counts[i] + addition
            spare = spare - addition
    return np.array(counts)


def bell_draw(key, extent, deviation, most, split=(), kind=jnp.bfloat16):
    level = steps_of(key, extent, split, -0.22, 0.18) if split else 1.0
    entries = jax.random.normal(key, extent, jnp.float32) * deviation * level
    return jnp.minimum(jnp.maximum(entries, -most), most).astype(kind)


def setup_inputs(seed: int = 0) -> dict:
    key_list = jax.random.split(jax.random.key(seed), 15)
    queries = draw_queries(jax.random.fold_in(key_list[14], 71), 0)
    new_key = bell_draw(key_list[1], (REQ, KVH * HD), 1.0, 5.0, ((0, 128), (1, 4)))
    new_value = bell_draw(key_list[2], (REQ, KVH * HD), 1.0, 5.0, ((0, 128), (1, 4)))
    cache_keys = draw_cache_keys(jax.random.fold_in(key_list[14], 71), 0)
    cache_values = bell_draw(key_list[4], (REQ, L, KVH * HD), 1.0, 5.0, ((0, 128), (2, 4)))
    lengths = draw_lengths(jax.random.fold_in(key_list[14], 71), 0)
    out_proj = bell_draw(key_list[6], (KVH, HQ // KVH * HD, D), (HQ * HD // 4) ** -0.5, 0.21875, ((0, 4), (1, 32), (2, 4)))
    residual = draw_residual(jax.random.fold_in(key_list[14], 71), 0)
    norm_gain = jnp.clip(1.0 + 0.15 * jax.random.normal(key_list[8], (D,), jnp.float32), 0.25, 1.75).astype(jnp.bfloat16)
    expert_ids_keys = jax.random.split(jax.random.fold_in(key_list[9], 1), REQ // REQ)
    expert_ids_turns = jax.random.permutation(jax.random.fold_in(key_list[9], 3), REQ // REQ)
    expert_ids = jax.vmap(lambda own, number: deal_out(jax.random.fold_in(key_list[9], 2), own, number, REQ, E, TOPK, CAP, 1))(expert_ids_keys, expert_ids_turns).reshape((REQ, TOPK))
    gate_weights = jnp.clip(jnp.exp(math.log(1.0) - 2.306499 * jax.random.uniform(key_list[10], (REQ, TOPK), jnp.float32) ** steps_of(key_list[10], (REQ, TOPK), ((0, 32),), -0.2, 0.2)), 0.099609375, 1.0).astype(jnp.bfloat16)
    gate_proj = bell_draw(key_list[11], (E, FF, D), D ** -0.5, 0.078125, ((0, 4), (1, 32), (2, 4)))
    up_proj = bell_draw(key_list[12], (E, FF, D), D ** -0.5, 0.078125, ((0, 4), (1, 32), (2, 4)))
    down_proj = bell_draw(key_list[13], (E, FF, D), (FF // 4) ** -0.5, 0.15625, ((0, 4), (1, 32), (2, 4)))
    return {"queries": queries, "new_key": new_key, "new_value": new_value, "cache_keys": cache_keys, "cache_values": cache_values, "lengths": lengths, "out_proj": out_proj, "residual": residual, "norm_gain": norm_gain, "expert_ids": expert_ids, "gate_weights": gate_weights, "gate_proj": gate_proj, "up_proj": up_proj, "down_proj": down_proj}


eps = 1e-05

def attend_block(queries, new_key, new_value, cache_keys, cache_values, lengths):
    count = queries.shape[0]
    heads_kv = new_key.shape[1] // HD
    group = queries.shape[1] // (heads_kv * HD)
    span = cache_keys.shape[1]
    query_rows_full = queries.reshape(count, heads_kv, group, HD).astype(jnp.float32)
    k_old = cache_keys.reshape(count, span, heads_kv, HD).astype(jnp.float32)
    v_old = cache_values.reshape(count, span, heads_kv, HD).astype(jnp.float32)
    incoming_key = new_key.reshape(count, heads_kv, HD).astype(jnp.float32)
    v_new = new_value.reshape(count, heads_kv, HD).astype(jnp.float32)
    multiplier = 1.0 / math.sqrt(HD)
    scores = jnp.einsum('bkgd,blkd->bkgl', query_rows_full, k_old) * multiplier
    self_score = jnp.einsum('zxlo,zxo->zxl', query_rows_full, incoming_key) * multiplier
    live = (jnp.arange(span)[None, :] < lengths[:, None])[:, None, None, :]
    scores = jnp.where(live, scores, -1e+30)
    highest = jnp.maximum(lax.optimization_barrier(jnp.max(scores, axis=-1)), self_score)
    expos = jnp.where(live, jnp.exp(scores - highest[..., None]), 0.0)
    own_exp = jnp.exp(self_score - highest)
    totals = lax.optimization_barrier(jnp.sum(expos, axis=-1)) + own_exp
    weights = (expos / totals[..., None]).astype(jnp.bfloat16)
    own_weight = (own_exp / totals).astype(jnp.bfloat16)
    summed = jnp.einsum('bkgl,blkd->bkgd', weights.astype(jnp.float32), v_old)
    summed = summed + own_weight.astype(jnp.float32)[..., None] * v_new[:, :, None, :]
    return summed.reshape(count, -1).astype(jnp.bfloat16)

def reference(queries, new_key, new_value, cache_keys, cache_values, lengths, out_proj, residual, norm_gain, expert_ids, gate_weights, gate_proj, up_proj, down_proj):
    blocks = REQ // 8

    def one_block(pieces):
        return attend_block(*pieces)
    attended = lax.map(one_block, (queries.reshape(blocks, 8, -1), new_key.reshape(blocks, 8, -1), new_value.reshape(blocks, 8, -1), cache_keys.reshape(blocks, 8, L, -1), cache_values.reshape(blocks, 8, L, -1), lengths.reshape(blocks, 8)))
    attended = attended.reshape(REQ, HQ * HD)
    projection = out_proj.reshape(HQ * HD, D)
    mixed = jnp.dot(attended, projection, preferred_element_type=jnp.float32)
    hidden = (residual.astype(jnp.float32) + mixed).astype(jnp.bfloat16)
    hidden_f = hidden.astype(jnp.float32)
    center = lax.optimization_barrier(jnp.sum(hidden_f, axis=1)) / D
    spread = lax.optimization_barrier(jnp.sum(hidden_f * hidden_f, axis=1)) / D - center * center
    normed = ((hidden_f - center[:, None]) * lax.rsqrt(spread + eps)[:, None] * norm_gain.astype(jnp.float32)[None, :]).astype(jnp.bfloat16)
    moe = jnp.zeros((REQ, D), jnp.float32)
    for expert in range(E):
        gate = jnp.dot(normed, gate_proj[expert].T, preferred_element_type=jnp.float32)
        upper = jnp.dot(normed, up_proj[expert].T, preferred_element_type=jnp.float32)
        active = (jax.nn.silu(gate) * upper).astype(jnp.bfloat16)
        result = jnp.dot(active, down_proj[expert], preferred_element_type=jnp.float32)
        share = lax.optimization_barrier(jnp.sum(jnp.where(expert_ids == expert, gate_weights.astype(jnp.float32), 0.0), axis=1))
        moe = moe + share[:, None] * result
    return (hidden_f + moe).astype(jnp.bfloat16)
```

```python
import functools
import math

import jax
import jax.numpy as jnp
from jax import lax
from jax.experimental import pallas as pl
from jax.experimental.pallas import tpu as pltpu
from jax.sharding import PartitionSpec as P

D = 6144
HD = 128
HG = 6
SPAN = 512
R = 3
EPS = 1e-05
NZ, NX = 16, 4
WD = D // NX
QW = WD // 4
KR = 24
KG = 768
F2 = 336
FC = 2 * F2
ZR = NZ * R
ROWS = NX * ZR
MESH = pl.DeviceIdType.MESH
BF = jnp.bfloat16
F32 = jnp.float32


def iota(shape, dim):
    return lax.broadcasted_iota(jnp.int32, shape, dim)


def onehot(cond):
    return jnp.where(cond, 1.0, 0.0).astype(BF)


def quotient(v, n):
    return (v * (65536 // n + 1)) >> 16


def mm(a, b):
    return jnp.dot(a, b, preferred_element_type=F32)


def mm_t(a, b):
    return lax.dot_general(a, b, (((1,), (1,)), ((), ())), preferred_element_type=F32)


def kernel(
    len_ref, q_ref, nk_ref, nv_ref, ck_ref, cv_ref, op_ref, res_ref, gain_ref, eid_ref, gw_ref,
    wg_ref, wu_ref, wd_ref,
    out_ref,
    wgu, wdn, w2, at, a2, xs, xr, st, hb, nm, gu, gr, ac, ms, mr, zs, zr,
    load_sem, wsend, wrecv, osend, orecv, csend, crecv, asend, arecv, xsend, xrecv, tsend, trecv,
    hsend, hrecv, fsend, frecv, gsend, grecv, bsend, brecv, msend, mrecv, zsend, zrecv,
):
    attn = lax.axis_index("attn")
    z, c = attn // 2, lax.rem(attn, 2)
    x, y = lax.axis_index("egrp"), lax.axis_index("eslice")

    def at_z(d):
        return (lax.rem(z + d + NZ, NZ) * 2 + c, x, y)

    def at_x(d):
        return (attn, lax.rem(x + d, NX), y)

    def at_y(d):
        return (attn, x, lax.rem(y + d, NX))

    sibling = (z * 2 + 1 - c, x, y)
    peers = [sibling]
    peers += [at_z(d) for d in range(1, NZ)]
    peers += [at_x(d) for d in range(1, NX)] + [at_y(d) for d in range(1, NX)]

    def send(src, dst, ssem, rsem, to):
        cp = pltpu.make_async_remote_copy(
            src_ref=src, dst_ref=dst, send_sem=ssem, recv_sem=rsem, device_id=to, device_id_type=MESH
        )
        cp.start()
        return cp

    def rows(ref, start, n):
        return ref.at[pl.ds(pl.multiple_of(start, 16), n)]

    barrier = pltpu.get_barrier_semaphore()
    for p in peers:
        pl.semaphore_signal(barrier, inc=1, device_id=p, device_id_type=MESH)

    loads = []
    for k, (src, dst, base) in enumerate(((wg_ref, wgu, 0), (wu_ref, wgu, FC), (wd_ref, wdn, 0))):
        cp = pltpu.make_async_copy(src, rows(dst, base + c * F2, F2), load_sem.at[k])
        cp.start()
        loads.append(cp)

    own = op_ref[...].astype(F32)
    block = jnp.concatenate([own[:, : WD // 2], own[:, WD // 2 :]], axis=0).astype(BF)
    w2[pl.ds(pl.multiple_of(attn * 2 * KR, 16), 2 * KR), :] = block

    with jax.named_scope("attention"):
        qf = q_ref[...].astype(F32)
        pad2 = jnp.zeros((2, HD), F32)
        pieces = []
        for r in range(R):
            pieces += [qf[r : r + 1, h * HD : (h + 1) * HD] for h in range(HG)] + [pad2]
        q24 = jnp.concatenate(pieces, axis=0)
        q32 = jnp.concatenate([q24, jnp.zeros((8, HD), F32)], axis=0).astype(BF)
        nk24 = jnp.concatenate([jnp.broadcast_to(nk_ref[r : r + 1, :].astype(F32), (8, HD)) for r in range(R)], 0)
        nv24 = jnp.concatenate([jnp.broadcast_to(nv_ref[r : r + 1, :].astype(F32), (8, HD)) for r in range(R)], 0)
        len24 = jnp.concatenate([jnp.full((8, 1), len_ref[r], jnp.int32) for r in range(R)], 0)
        scale = 1.0 / math.sqrt(HD)
        scores = jnp.concatenate([mm_t(q32, ck_ref[r])[r * 8 : (r + 1) * 8] for r in range(R)], 0) * scale
        self_score = jnp.sum(q24 * nk24, axis=1, keepdims=True) * scale
        live = iota((R * 8, SPAN), 1) < len24
        scores = jnp.where(live, scores, -1e30)
        highest = jnp.maximum(jnp.max(scores, axis=1, keepdims=True), self_score)
        expos = jnp.where(live, jnp.exp(scores - highest), 0.0)
        own_exp = jnp.exp(self_score - highest)
        totals = jnp.sum(expos, axis=1, keepdims=True) + own_exp
        weights = jnp.concatenate([expos / totals, jnp.zeros((8, SPAN), F32)], axis=0).astype(BF)
        own_weight = (own_exp / totals).astype(BF).astype(F32)
        summed = jnp.concatenate([mm(weights, cv_ref[r])[r * 8 : (r + 1) * 8] for r in range(R)], 0)
        summed = summed + own_weight * nv24
        at[pl.ds(pl.multiple_of(y * 32, 16), 32), :] = jnp.concatenate(
            [summed, jnp.zeros((8, HD), F32)], axis=0
        ).astype(BF)

    with jax.named_scope("entry"):
        pl.semaphore_wait(barrier, len(peers))

    sends = []
    a_cps = []
    mine = rows(at, y * 32, 32)
    for d in range(1, NX):
        a_cps.append(send(mine, mine, asend.at[d - 1], arecv.at[d - 1], at_y(d)))
    o_cps = {}
    c_cps = []

    def block_of(d):
        return rows(w2, (lax.rem(z - d + 2 * NZ, NZ) * 2 + c) * 2 * KR, 2 * KR)

    def pass_on(d, sign):
        for s in (2, 1):
            far = d + s
            if far > (NZ // 2 if sign > 0 else NZ // 2 - 1):
                continue
            k = far - 1 if sign > 0 else NZ // 2 + far - 1
            o_cps[sign * far] = send(
                block_of(sign * d), block_of(sign * d), osend.at[k], orecv.at[k], at_z(sign * s)
            )

    def to_sibling(d):
        k = d + NZ // 2 - 1
        c_cps.append(send(block_of(d), block_of(d), csend.at[k], crecv.at[k], sibling))

    pass_on(0, 1)
    pass_on(0, -1)
    to_sibling(0)
    w_cps = []
    for k, (src, dst, base) in enumerate(((wg_ref, wgu, 0), (wu_ref, wgu, FC), (wd_ref, wdn, 0))):
        w_cps.append(send(src, rows(dst, base + c * F2, F2), wsend.at[k], wrecv.at[k], sibling))

    row16, lane16 = iota((16, 4 * R), 0), iota((16, 4 * R), 1)
    part = row16 & 3
    wanted = (lane16 == x * R + part) & (part < R)
    res16 = jnp.zeros((16, QW), F32)
    for q in range(4):
        res16 = res16 + mm(onehot(wanted & ((row16 >> 2) == q)), res_ref[:, q * QW : (q + 1) * QW])
    gain16 = jnp.concatenate(
        [jnp.broadcast_to(gain_ref[:, q * QW : (q + 1) * QW].astype(F32), (4, QW)) for q in range(4)], 0
    )
    first = (iota((4 * R, 128), 0) - x * R) * 8
    share_row = jnp.zeros((1, 128), F32)
    lane12 = iota((4 * R, 128), 1)
    gwf = gw_ref[...].astype(F32)
    for k in range(4):
        hit = (lane12 == first + eid_ref[:, k : k + 1]) & (first >= 0) & (first < 8 * R)
        share_row = share_row + jnp.sum(jnp.where(hit, gwf[:, k : k + 1], 0.0), axis=0, keepdims=True)

    with jax.named_scope("attended_gather"):
        for cp in a_cps:
            cp.wait_recv()
        p, s = iota((HG * 16, 128), 0), iota((HG * 16, 128), 1)
        pick = onehot(s == ((p >> 2) & 3) * 32 + (p & 3) * 8 + (p >> 4))
        heads = mm(pick, at[...]).astype(BF)
        a16 = jnp.concatenate([heads[h * 16 : (h + 1) * 16] for h in range(HG)], axis=1)
        j = iota((1, 2 * KG), 1)
        blk = quotient(j, 2 * KR)
        rem = j - blk * 2 * KR
        second = rem >= KR
        source = blk * KR + jnp.where(second, rem - KR, rem)
        n = 512
        for t in range(2 * KG // n):
            cols = slice(t * n, (t + 1) * n)
            spread_out = mm(a16, onehot(iota((KG, n), 0) == source[:, cols]))
            later = second[:, cols]
            a2[:, cols] = jnp.concatenate(
                [jnp.where(later, 0.0, spread_out), jnp.where(later, spread_out, 0.0)], axis=0
            ).astype(BF)

    with jax.named_scope("projection_gather"):
        for d in range(1, NZ // 2 + 1):
            for sign in (1, -1):
                if sign * d not in o_cps:
                    continue
                o_cps[sign * d].wait_recv()
                if d % 2 == 0:
                    pass_on(d, sign)
                to_sibling(sign * d)
        for cp in c_cps:
            cp.wait_recv()

    with jax.named_scope("projection"):
        mixed = jnp.zeros((32, WD // 2), F32)
        for t in range(4):
            n = 2 * KG // 4
            mixed = mixed + mm(a2[:, t * n : (t + 1) * n], w2[t * n : (t + 1) * n, :])
        mixed = mixed.astype(BF)
        p, s = iota((64, 32), 0), iota((64, 32), 1)
        source = (((p >> 3) & 1) << 4) + ((p >> 4) << 2) + (p & 3)
        odd = ((p >> 2) & 1) == 1
        xs[...] = (
            mm(onehot((s == source) & ~odd), mixed[:, :QW]) + mm(onehot((s == source) & odd), mixed[:, QW:])
        ).astype(BF)

    with jax.named_scope("projection_terms"):
        cps = []
        for d in range(1, NX):
            to = lax.rem(x + d, NX)
            cps.append(send(rows(xs, to * 16, 16), rows(xr, x * 16, 16), xsend.at[d - 1], xrecv.at[d - 1], at_x(d)))
        for cp in cps:
            cp.wait_recv()
        sends += cps
        xr[pl.ds(pl.multiple_of(x * 16, 16), 16), :] = xs[pl.ds(pl.multiple_of(x * 16, 16), 16), :]
        terms = xr[...].astype(F32)
        hidden = res16 + ((terms[0:16] + terms[16:32]) + (terms[32:48] + terms[48:64]))
        hidden = hidden.astype(BF).astype(F32)

    with jax.named_scope("layer_norm"):
        lane = iota((16, 128), 1)
        s1 = jnp.sum(hidden, axis=1, keepdims=True)
        s2 = jnp.sum(hidden * hidden, axis=1, keepdims=True)
        mine = rows(st, y * 16, 16)
        st[pl.ds(pl.multiple_of(y * 16, 16), 16), :] = jnp.where(lane == 0, s1, jnp.where(lane == 1, s2, 0.0))
        cps = [send(mine, mine, tsend.at[d - 1], trecv.at[d - 1], at_y(d)) for d in range(1, NX)]
        for cp in cps:
            cp.wait_recv()
        sends += cps
        stats = st[...]
        stats = (stats[0:16] + stats[16:32]) + (stats[32:48] + stats[48:64])
        stats = stats[0:8] + stats[8:16]
        stats = stats[0:4] + stats[4:8]
        stats = jnp.concatenate([stats] * 4, axis=0)
        center = stats[:, 0:1] / D
        spread = stats[:, 1:2] / D - center * center
        normed = (hidden - center) * lax.rsqrt(spread + EPS) * gain16
        pad = (iota((16, QW), 0) & 3) == 3
        extra = jnp.concatenate([share_row, jnp.zeros((1, QW - 128), F32)], axis=1)
        extra = jnp.where(iota((16, QW), 0) == 3, extra, 0.0)
        hb[pl.ds(pl.multiple_of((x * NZ + z) * 16, 16), 16), :] = jnp.where(pad, extra, normed).astype(BF)

    with jax.named_scope("token_gather"):
        f_cps = []

        def over_x(d):
            blk = rows(hb, (x * NZ + lax.rem(z - d + NZ, NZ)) * 16, 16)
            for k in range(1, NX):
                n = (k - 1) * NZ + d
                f_cps.append(send(blk, blk, fsend.at[n], frecv.at[n], at_x(k)))

        blk = rows(hb, (x * NZ + z) * 16, 16)
        order = [8] + [v for i in range(7, 0, -1) for v in (i, NZ - i)]
        h_cps = {d: send(blk, blk, hsend.at[d], hrecv.at[d], at_z(d)) for d in order}
        over_x(0)
        for d in sorted(order, key=lambda v: min(v, NZ - v)):
            h_cps[d].wait_recv()
            over_x(d)
        for cp in f_cps:
            cp.wait_recv()

    with jax.named_scope("compact"):
        p, s = iota((4 * ZR, NZ * 16), 0), iota((4 * ZR, NZ * 16), 1)
        quarter = quotient(p, ZR)
        m = p - quarter * ZR
        who = quotient(m, R)
        pick = onehot(s == who * 16 + quarter * 4 + (m - who * R))
        for g in range(NX):
            got = mm(pick, hb[g * NZ * 16 : (g + 1) * NZ * 16, :]).astype(BF)
            for q in range(4):
                nm[g * ZR : (g + 1) * ZR, q * QW : (q + 1) * QW] = got[q * ZR : (q + 1) * ZR]
        p, s = iota((ZR, NZ * 16), 0), iota((ZR, NZ * 16), 1)
        who = quotient(p, R)
        shares = mm(onehot(s == who * 16 + 3), hb[pl.ds(pl.multiple_of(y * NZ * 16, 16), NZ * 16), 0:128])
        lane = iota((ZR, 128), 1)
        place = (iota((ZR, 128), 0) - quotient(iota((ZR, 128), 0), R) * R) * 8 + x * 2
        share0 = jnp.sum(jnp.where(lane == place, shares, 0.0), axis=1, keepdims=True)
        share1 = jnp.sum(jnp.where(lane == place + 1, shares, 0.0), axis=1, keepdims=True)

    with jax.named_scope("gate_up"):
        for cp in loads:
            cp.wait()
        for cp in w_cps:
            cp.wait_recv()
        tokens = nm[...]
        for lo, hi in ((0, 512), (512, 1024), (1024, 2 * FC)):
            gu[:, lo:hi] = mm_t(tokens, wgu[lo:hi, :]).astype(BF)

    with jax.named_scope("gate_up_terms"):
        cps = []
        for d in range(1, NX):
            to = lax.rem(y + d, NX)
            cps.append(send(rows(gu, to * ZR, ZR), rows(gr, y * ZR, ZR), gsend.at[d - 1], grecv.at[d - 1], at_y(d)))
        for cp in cps:
            cp.wait_recv()
        sends += cps
        gr[pl.ds(pl.multiple_of(y * ZR, 16), ZR), :] = gu[pl.ds(pl.multiple_of(y * ZR, 16), ZR), :]

    with jax.named_scope("activation"):
        total = gr[0:ZR, :].astype(F32)
        for g in range(1, NX):
            total = total + gr[g * ZR : (g + 1) * ZR, :].astype(F32)
        gate, up = total[:, :FC], total[:, FC:]
        unit = iota((ZR, FC), 1)
        unit = jnp.where(unit >= F2, unit - F2, unit)
        share = jnp.where(unit >= F2 // 2, share1, share0)
        mine = rows(ac, y * ZR, ZR)
        ac[pl.ds(pl.multiple_of(y * ZR, 16), ZR), :] = (gate / (1.0 + jnp.exp(-gate)) * up * share).astype(BF)

    with jax.named_scope("activation_gather"):
        cps = [send(mine, mine, bsend.at[d - 1], brecv.at[d - 1], at_y(d)) for d in range(1, NX)]
        for cp in cps:
            cp.wait_recv()
        sends += cps

    with jax.named_scope("down"):
        act = ac[...]
        for t in range(3):
            n = WD // 3
            ms[:, t * n : (t + 1) * n] = mm(act, wdn[:, t * n : (t + 1) * n]).astype(BF)

    with jax.named_scope("expert_sum_x"):
        cps = []
        for d in range(1, NX):
            to = lax.rem(x + d, NX)
            cps.append(send(rows(ms, to * ZR, ZR), rows(mr, x * ZR, ZR), msend.at[d - 1], mrecv.at[d - 1], at_x(d)))
        for cp in cps:
            cp.wait_recv()
        sends += cps
        mr[pl.ds(pl.multiple_of(x * ZR, 16), ZR), :] = ms[pl.ds(pl.multiple_of(x * ZR, 16), ZR), :]
        total = mr[0:ZR, :].astype(F32)
        for g in range(1, NX):
            total = total + mr[g * ZR : (g + 1) * ZR, :].astype(F32)
        total = total.astype(BF)
        p, s = iota((NZ * 16, ZR), 0), iota((NZ * 16, ZR), 1)
        wanted = (s == (p >> 4) * R + (p & 3)) & ((p & 3) < R)
        piece = jnp.zeros((NZ * 16, QW), F32)
        for q in range(4):
            piece = piece + mm(onehot(wanted & (((p >> 2) & 3) == q)), total[:, q * QW : (q + 1) * QW])
        zs[...] = piece.astype(BF)

    with jax.named_scope("expert_sum_z"):
        cps = []
        for d in order:
            to = lax.rem(z + d, NZ)
            cps.append(send(rows(zs, to * 16, 16), rows(zr, z * 16, 16), zsend.at[d], zrecv.at[d], at_z(d)))
        for cp in cps:
            cp.wait_recv()
        sends += cps
        zr[pl.ds(pl.multiple_of(z * 16, 16), 16), :] = zs[pl.ds(pl.multiple_of(z * 16, 16), 16), :]
        total = hidden
        for g in range(NZ):
            total = total + zr[g * 16 : (g + 1) * 16, :].astype(F32)
        for q in range(4):
            out_ref[:, q * QW : (q + 1) * QW] = total[q * 4 : q * 4 + R, :].astype(BF)

    with jax.named_scope("drain"):
        for cp in a_cps + list(o_cps.values()) + c_cps + w_cps + list(h_cps.values()) + f_cps + sends:
            cp.wait_send()


def on_device(
    queries, new_key, new_value, cache_keys, cache_values, lengths, out_proj, residual, norm_gain,
    expert_ids, gate_weights, gate_proj, up_proj, down_proj,
):
    vmem = pl.BlockSpec(memory_space=pltpu.VMEM)
    dma = pltpu.SemaphoreType.DMA
    return pl.pallas_call(
        kernel,
        out_shape=jax.ShapeDtypeStruct((R, WD), BF),
        in_specs=[pl.BlockSpec(memory_space=pltpu.SMEM)] + [vmem] * 10 + [pl.BlockSpec(memory_space=pl.ANY)] * 3,
        out_specs=vmem,
        scratch_shapes=[
            pltpu.VMEM((2 * FC, WD), BF),
            pltpu.VMEM((FC, WD), BF),
            pltpu.VMEM((2 * KG, WD // 2), BF),
            pltpu.VMEM((NX * 32, HD), BF),
            pltpu.VMEM((32, 2 * KG), BF),
            pltpu.VMEM((64, QW), BF),
            pltpu.VMEM((64, QW), BF),
            pltpu.VMEM((64, 128), F32),
            pltpu.VMEM((NX * NZ * 16, QW), BF),
            pltpu.VMEM((ROWS, WD), BF),
            pltpu.VMEM((ROWS, 2 * FC), BF),
            pltpu.VMEM((ROWS, 2 * FC), BF),
            pltpu.VMEM((ROWS, FC), BF),
            pltpu.VMEM((ROWS, WD), BF),
            pltpu.VMEM((ROWS, WD), BF),
            pltpu.VMEM((NZ * 16, QW), BF),
            pltpu.VMEM((NZ * 16, QW), BF),
            dma((3,)),
            dma((3,)), dma((3,)),
            dma((NZ,)), dma((NZ,)),
            dma((NZ,)), dma((NZ,)),
            dma((3,)), dma((3,)),
            dma((3,)), dma((3,)),
            dma((3,)), dma((3,)),
            dma((NZ,)), dma((NZ,)),
            dma((3 * NZ,)), dma((3 * NZ,)),
            dma((3,)), dma((3,)),
            dma((3,)), dma((3,)),
            dma((3,)), dma((3,)),
            dma((NZ,)), dma((NZ,)),
        ],
        compiler_params=pltpu.CompilerParams(
            collective_id=0, has_side_effects=True, vmem_limit_bytes=48 << 20
        ),
        name="decode_layer",
    )(
        lengths, queries, new_key, new_value, cache_keys, cache_values,
        out_proj.reshape(KR, WD), residual, norm_gain.reshape(1, WD), expert_ids, gate_weights,
        gate_proj.reshape(F2, WD), up_proj.reshape(F2, WD), down_proj.reshape(F2, WD),
    )


def solution(mesh):
    placed = (
        P(("attn", "eslice"), "egrp"),
        P(("attn", "eslice"), "egrp"),
        P(("attn", "eslice"), "egrp"),
        P(("attn", "eslice"), None, "egrp"),
        P(("attn", "eslice"), None, "egrp"),
        P(("attn", "eslice")),
        P("egrp", "attn", "eslice"),
        P("attn", "eslice"),
        P("eslice"),
        P("attn", None),
        P("attn", None),
        P("egrp", "attn", "eslice"),
        P("egrp", "attn", "eslice"),
        P("egrp", "attn", "eslice"),
    )
    return jax.shard_map(
        on_device, mesh=mesh, in_specs=placed, out_specs=P(("attn", "egrp"), "eslice"), check_vma=False
    )
```

```python
import functools
import math

import jax
import jax.numpy as jnp
from jax import lax
from jax.experimental import pallas as pl
from jax.experimental.pallas import tpu as pltpu
from jax.sharding import PartitionSpec as P

D = 6144
HD = 128
HG = 6
SPAN = 512
R = 3
EPS = 1e-05
NZ, NX = 16, 4
WD = D // NX
QW = WD // 4
KR = 24
KG = 768
F2 = 336
FC = 2 * F2
ZR = NZ * R
GW = 2 * FC + 64
ROWS = NX * ZR
MESH = pl.DeviceIdType.MESH
BF = jnp.bfloat16
F32 = jnp.float32


def iota(shape, dim):
    return lax.broadcasted_iota(jnp.int32, shape, dim)


def onehot(cond):
    return jnp.where(cond, 1.0, 0.0).astype(BF)


def quotient(v, n):
    return (v * (65536 // n + 1)) >> 16


def mm(a, b):
    return jnp.dot(a, b, preferred_element_type=F32)


def mm_t(a, b):
    return lax.dot_general(a, b, (((1,), (1,)), ((), ())), preferred_element_type=F32)


def kernel(
    len_ref, q_hbm, nk_hbm, nv_hbm, ck_hbm, cv_hbm, op_hbm, res_hbm, gain_hbm, eid_hbm, gw_hbm,
    wg_ref, wu_ref, wd_ref,
    out_ref,
    qv, nkv, nvv, ckv, cvv, opv, resv, gainv, eidv, gwv, wgu, wdn, w2, at, a2, xs, xr, gs, hb, nm, gu, gr, ac, ms, mr, zs, zr,
    load_sem, wsend, wrecv, osend, orecv, csend, crecv, asend, arecv, xsend, xrecv, tsend, trecv,
    hsend, hrecv, fsend, frecv, gsend, grecv, bsend, brecv, msend, mrecv, zsend, zrecv,
):
    attn = lax.axis_index("attn")
    z, c = attn // 2, lax.rem(attn, 2)
    x, y = lax.axis_index("egrp"), lax.axis_index("eslice")

    def at_z(d):
        return (lax.rem(z + d + NZ, NZ) * 2 + c, x, y)

    def at_x(d):
        return (attn, lax.rem(x + d, NX), y)

    def at_y(d):
        return (attn, x, lax.rem(y + d, NX))

    quad, seat = z // 4, lax.rem(z, 4)

    def in_quad(s, dx, dy):
        return ((quad * 4 + s) * 2 + c, lax.rem(x + dx, NX), lax.rem(y + dy, NX))

    sibling = (z * 2 + 1 - c, x, y)
    others = [(k // 4, k % 4) for k in range(1, 16)]
    peers = [sibling]
    peers += [at_z(d) for d in range(1, NZ)]
    peers += [at_x(d) for d in range(1, NX)] + [at_y(d) for d in range(1, NX)]
    peers += [in_quad(lax.rem(seat + k, 4), m, 0) for k, m in others if k and m]
    peers += [in_quad(lax.rem(seat + k, 4), 0, m) for k, m in others if k and m]

    def send(src, dst, ssem, rsem, to):
        cp = pltpu.make_async_remote_copy(
            src_ref=src, dst_ref=dst, send_sem=ssem, recv_sem=rsem, device_id=to, device_id_type=MESH
        )
        cp.start()
        return cp

    def rows(ref, start, n):
        return ref.at[pl.ds(pl.multiple_of(start, 16), n)]

    barrier = pltpu.get_barrier_semaphore()
    for p in peers:
        pl.semaphore_signal(barrier, inc=1, device_id=p, device_id_type=MESH)

    def load(src, dst, sem):
        cp = pltpu.make_async_copy(src, dst, sem)
        cp.start()
        return cp

    l_q, l_nk, l_nv, l_ck, l_cv, l_op = [
        load(src, dst, load_sem.at[k])
        for k, (src, dst) in enumerate(
            ((q_hbm, qv), (nk_hbm, nkv), (nv_hbm, nvv), (ck_hbm, ckv), (cv_hbm, cvv), (op_hbm, opv))
        )
    ]
    l_rest = [
        load(src, dst, load_sem.at[k + 6])
        for k, (src, dst) in enumerate(((res_hbm, resv), (gain_hbm, gainv), (eid_hbm, eidv), (gw_hbm, gwv)))
    ]
    expert_weights = ((wg_ref, wgu, 0), (wu_ref, wgu, FC), (wd_ref, wdn, 0))
    loads = [
        load(src, rows(dst, base + c * F2, F2), load_sem.at[k + 10])
        for k, (src, dst, base) in enumerate(expert_weights)
    ]

    l_op.wait()
    own = opv[...].astype(F32)
    block = jnp.concatenate([own[:, : WD // 2], own[:, WD // 2 :]], axis=0).astype(BF)
    w2[pl.ds(pl.multiple_of((quad * 2 + c) * 2 * KR, 16), 2 * KR), :] = block

    with jax.named_scope("attention"):
        for cp in (l_q, l_nk, l_nv, l_ck, l_cv):
            cp.wait()
        qf = qv[...].astype(F32)
        pad2 = jnp.zeros((2, HD), F32)
        pieces = []
        for r in range(R):
            pieces += [qf[r : r + 1, h * HD : (h + 1) * HD] for h in range(HG)] + [pad2]
        q24 = jnp.concatenate(pieces, axis=0)
        q32 = jnp.concatenate([q24, jnp.zeros((8, HD), F32)], axis=0).astype(BF)
        nk24 = jnp.concatenate([jnp.broadcast_to(nkv[r : r + 1, :].astype(F32), (8, HD)) for r in range(R)], 0)
        nv24 = jnp.concatenate([jnp.broadcast_to(nvv[r : r + 1, :].astype(F32), (8, HD)) for r in range(R)], 0)
        len24 = jnp.concatenate([jnp.full((8, 1), len_ref[r], jnp.int32) for r in range(R)], 0)
        scale = 1.0 / math.sqrt(HD)
        scores = jnp.concatenate([mm_t(q32, ckv[r])[r * 8 : (r + 1) * 8] for r in range(R)], 0) * scale
        self_score = jnp.sum(q24 * nk24, axis=1, keepdims=True) * scale
        live = iota((R * 8, SPAN), 1) < len24
        scores = jnp.where(live, scores, -1e30)
        highest = jnp.maximum(jnp.max(scores, axis=1, keepdims=True), self_score)
        expos = jnp.where(live, jnp.exp(scores - highest), 0.0)
        own_exp = jnp.exp(self_score - highest)
        totals = jnp.sum(expos, axis=1, keepdims=True) + own_exp
        weights = jnp.concatenate([expos / totals, jnp.zeros((8, SPAN), F32)], axis=0).astype(BF)
        own_weight = (own_exp / totals).astype(BF).astype(F32)
        summed = jnp.concatenate([mm(weights, cvv[r])[r * 8 : (r + 1) * 8] for r in range(R)], 0)
        summed = summed + own_weight * nv24
        at[pl.ds(pl.multiple_of((seat * 4 + y) * 32, 16), 32), :] = jnp.concatenate(
            [summed, jnp.zeros((8, HD), F32)], axis=0
        ).astype(BF)

    with jax.named_scope("entry"):
        pl.semaphore_wait(barrier, len(peers))

    sends = []
    def block_of(d):
        return rows(w2, (lax.rem(quad - d + 4, 4) * 2 + c) * 2 * KR, 2 * KR)

    o_cps = {d: send(block_of(0), block_of(0), osend.at[d], orecv.at[d], at_z(4 * d)) for d in (2, 1, 3)}
    c_cps = [send(block_of(0), block_of(0), csend.at[0], crecv.at[0], sibling)]
    mine = rows(at, (seat * 4 + y) * 32, 32)
    a_cps = [
        send(mine, mine, asend.at[k * 4 + m], arecv.at[k * 4 + m], in_quad(lax.rem(seat + k, 4), 0, m))
        for k, m in others
    ]
    w_cps = []
    for k, (src, dst, base) in enumerate(expert_weights):
        w_cps.append(send(src, rows(dst, base + c * F2, F2), wsend.at[k], wrecv.at[k], sibling))

    for cp in l_rest:
        cp.wait()
    row16, lane16 = iota((16, 4 * R), 0), iota((16, 4 * R), 1)
    part = row16 & 3
    wanted = (lane16 == x * R + part) & (part < R)
    res16 = jnp.zeros((16, QW), F32)
    for q in range(4):
        res16 = res16 + mm(onehot(wanted & ((row16 >> 2) == q)), resv[:, q * QW : (q + 1) * QW])
    gain_row = gainv[...].reshape(1, WD)
    gain16 = jnp.concatenate(
        [jnp.broadcast_to(gain_row[:, q * QW : (q + 1) * QW].astype(F32), (4, QW)) for q in range(4)], 0
    )
    gwf = gwv[...].astype(F32)
    expert = iota((128, 4 * R), 0)
    shares = jnp.zeros((128, 4 * R), F32)
    for k in range(4):
        shares = shares + jnp.where(expert == eidv[k : k + 1, :], gwf[k : k + 1, :], 0.0)
    share16 = mm_t(onehot(lane16 == x * R + (row16 >> 2)), shares.astype(BF))

    with jax.named_scope("attended_gather"):
        for cp in a_cps:
            cp.wait_recv()
        p, s = iota((HG * 64, 512), 0), iota((HG * 64, 512), 1)
        pick = onehot(s == ((p & 63) >> 2) * 32 + (p & 3) * 8 + (p >> 6))
        heads = mm(pick, at[...]).astype(BF)
        a64 = jnp.concatenate([heads[h * 64 : (h + 1) * 64] for h in range(HG)], axis=1)
        j = iota((1, 16 * KR), 1)
        slot = quotient(j, 2 * KR)
        rem = j - slot * 2 * KR
        later = rem >= KR
        source = (((slot >> 1) * 4 + seat) * 2 + (slot & 1)) * KR + jnp.where(later, rem - KR, rem)
        wide = mm(a64, onehot(iota((KG, 16 * KR), 0) == source))
        a2[...] = jnp.concatenate([jnp.where(later, 0.0, wide), jnp.where(later, wide, 0.0)], axis=0).astype(BF)

    with jax.named_scope("projection_gather"):
        for d in (1, 3, 2):
            o_cps[d].wait_recv()
            c_cps.append(send(block_of(d), block_of(d), csend.at[d], crecv.at[d], sibling))

    with jax.named_scope("gain_sums"):
        for cp in loads:
            cp.wait()
        for cp in w_cps:
            cp.wait_recv()
        gains = jnp.broadcast_to(gain_row, (16, WD))
        for lo, hi in ((0, 512), (512, 1024), (1024, 2 * FC)):
            gs[pl.ds(pl.multiple_of(y * 8, 8), 8), lo:hi] = mm_t(gains, wgu[lo:hi, :])[0:8]
        mine = gs.at[pl.ds(pl.multiple_of(y * 8, 8), 8)]
        g_cps = [send(mine, mine, tsend.at[d - 1], trecv.at[d - 1], at_y(d)) for d in range(1, NX)]

    with jax.named_scope("projection"):
        for cp in c_cps:
            cp.wait_recv()
        mixed = mm(a2[...], w2[...]).astype(BF)
        p, s = iota((256, 128), 0), iota((256, 128), 1)
        source = (((p >> 3) & 1) << 6) + ((p >> 4) << 2) + (p & 3)
        odd = ((p >> 2) & 1) == 1
        xs[...] = (
            mm(onehot((s == source) & ~odd), mixed[:, :QW]) + mm(onehot((s == source) & odd), mixed[:, QW:])
        ).astype(BF)

    with jax.named_scope("projection_terms"):
        slot = (seat * 4 + x) * 16
        cps = []
        for k, m in others:
            to = lax.rem(seat + k, 4)
            n = k * 4 + m
            cps.append(
                send(
                    rows(xs, (to * 4 + lax.rem(x + m, NX)) * 16, 16), rows(xr, slot, 16),
                    xsend.at[n], xrecv.at[n], in_quad(to, m, 0),
                )
            )
        for cp in cps:
            cp.wait_recv()
        sends += cps
        xr[pl.ds(pl.multiple_of(slot, 16), 16), :] = xs[pl.ds(pl.multiple_of(slot, 16), 16), :]
        hidden = res16
        for g in range(16):
            hidden = hidden + xr[g * 16 : (g + 1) * 16, :].astype(F32)
        hidden = hidden.astype(BF).astype(F32)

    with jax.named_scope("center_slice"):
        def per_request(v):
            v = jnp.sum(v, axis=1, keepdims=True)
            v = v[0:8] + v[8:16]
            v = v[0:4] + v[4:8]
            return jnp.concatenate([v] * 4, axis=0)

        def halves(v):
            high = v.astype(BF).astype(F32)
            return high, v - high

        mean = (per_request(hidden) / WD).astype(BF).astype(F32)
        inside = (iota((16, QW), 0) & 3) < R
        near = jnp.where(inside, hidden - mean, 0.0)
        notes = (mean,) + halves(per_request(near)) + halves(per_request(near * near))
        lane = iota((16, 128), 1)
        row = iota((16, 128), 0)
        extra = jnp.where(lane < 8, share16, 0.0)
        for j, note in enumerate(notes):
            by_request = jnp.concatenate([jnp.broadcast_to(note[i : i + 1], (4, 1)) for i in range(4)], axis=0)
            extra = extra + jnp.where(lane == 8 + j, by_request, 0.0)
        extra = jnp.where((row & 3) == R, extra, 0.0)
        extra = jnp.concatenate([extra, jnp.zeros((16, QW - 128), F32)], axis=1)
        hb[pl.ds(pl.multiple_of((x * NZ + z) * 16, 16), 16), :] = (near * gain16 + extra).astype(BF)

    with jax.named_scope("token_gather"):
        f_cps = []

        def over_x(d):
            blk = rows(hb, (x * NZ + lax.rem(z - d + NZ, NZ)) * 16, 16)
            for k in (2, 1, 3):
                n = (k - 1) * NZ + d % NZ
                f_cps.append(send(blk, blk, fsend.at[n], frecv.at[n], at_x(k)))

        blk = rows(hb, (x * NZ + z) * 16, 16)
        h_cps = {}
        for d in (4, -4, 3, -3, 2, -2, 1, -1):
            h_cps[d] = send(blk, blk, hsend.at[d % NZ], hrecv.at[d % NZ], at_z(d))
        over_x(0)
        for sign in (1, -1):
            h_cps[sign * 4].wait_recv()
            blk = rows(hb, (x * NZ + lax.rem(z - sign * 4 + NZ, NZ)) * 16, 16)
            for s in (4, 3, 2, 1) if sign > 0 else (3, 2, 1):
                n = sign * (4 + s)
                h_cps[n] = send(blk, blk, hsend.at[n % NZ], hrecv.at[n % NZ], at_z(sign * s))
        for d in (4, -4):
            over_x(d)
        for d in (1, -1, 2, -2, 3, -3, 5, -5, 6, -6, 7, -7, 8):
            h_cps[d].wait_recv()
            over_x(d)
        for cp in f_cps:
            cp.wait_recv()

    with jax.named_scope("compact"):
        p, s = iota((4 * ZR, NZ * 16), 0), iota((4 * ZR, NZ * 16), 1)
        quarter = quotient(p, ZR)
        m = p - quarter * ZR
        who = quotient(m, R)
        pick = onehot(s == who * 16 + quarter * 4 + (m - who * R))
        for g in range(NX):
            got = mm(pick, hb[g * NZ * 16 : (g + 1) * NZ * 16, :]).astype(BF)
            for q in range(4):
                nm[g * ZR : (g + 1) * ZR, q * QW : (q + 1) * QW] = got[q * ZR : (q + 1) * ZR]
        p, s = iota((ZR, NZ * 16), 0), iota((ZR, NZ * 16), 1)
        who = quotient(p, R)
        pick = onehot(s == who * 16 + (p - who * R) * 4 + R)
        for g in range(NX):
            gu[g * ZR : (g + 1) * ZR, 2 * FC : 2 * FC + 16] = mm(
                pick, hb[g * NZ * 16 : (g + 1) * NZ * 16, 0:128]
            )[:, 0:16].astype(BF)

    with jax.named_scope("gate_up"):
        tokens = nm[...]
        for lo, hi in ((0, 512), (512, 1024), (1024, 2 * FC)):
            gu[:, lo:hi] = mm_t(tokens, wgu[lo:hi, :]).astype(BF)

    with jax.named_scope("gate_up_terms"):
        cps = []
        for d in range(1, NX):
            to = lax.rem(y + d, NX)
            cps.append(send(rows(gu, to * ZR, ZR), rows(gr, y * ZR, ZR), gsend.at[d - 1], grecv.at[d - 1], at_y(d)))
        for cp in cps:
            cp.wait_recv()
        sends += cps + g_cps
        gr[pl.ds(pl.multiple_of(y * ZR, 16), ZR), :] = gu[pl.ds(pl.multiple_of(y * ZR, 16), ZR), :]

    with jax.named_scope("activation"):
        total = gr[0:ZR, :].astype(F32)
        for g in range(1, NX):
            total = total + gr[g * ZR : (g + 1) * ZR, :].astype(F32)
        for cp in g_cps:
            cp.wait_recv()
        notes = [gr[g * ZR : (g + 1) * ZR, 2 * FC : 2 * FC + 16].astype(F32) for g in range(NX)]
        means = [n[:, 8:9] for n in notes]
        sums = [n[:, 9:10] + n[:, 10:11] for n in notes]
        squares = [n[:, 11:12] + n[:, 12:13] for n in notes]
        center = sum(s + WD * m for s, m in zip(sums, means)) / D
        apart = [m - center for m in means]
        spread = sum(q + 2.0 * a * s + WD * a * a for q, a, s in zip(squares, apart, sums)) / D
        whole = total[:, : 2 * FC]
        for g in range(NX):
            whole = whole + apart[g] * gs[g * 8 : g * 8 + 1, :]
        whole = whole * lax.rsqrt(spread + EPS)
        lane = iota((ZR, 16), 1)
        share0 = jnp.sum(jnp.where(lane == x * 2, notes[0], 0.0), axis=1, keepdims=True)
        share1 = jnp.sum(jnp.where(lane == x * 2 + 1, notes[0], 0.0), axis=1, keepdims=True)
        gate, up = whole[:, :FC], whole[:, FC:]
        unit = iota((ZR, FC), 1)
        unit = jnp.where(unit >= F2, unit - F2, unit)
        share = jnp.where(unit >= F2 // 2, share1, share0)
        mine = rows(ac, y * ZR, ZR)
        ac[pl.ds(pl.multiple_of(y * ZR, 16), ZR), :] = (gate / (1.0 + jnp.exp(-gate)) * up * share).astype(BF)

    with jax.named_scope("activation_gather"):
        cps = [send(mine, mine, bsend.at[d - 1], brecv.at[d - 1], at_y(d)) for d in range(1, NX)]
        for cp in cps:
            cp.wait_recv()
        sends += cps

    with jax.named_scope("down"):
        act = ac[...]
        for t in range(3):
            n = WD // 3
            ms[:, t * n : (t + 1) * n] = mm(act, wdn[:, t * n : (t + 1) * n]).astype(BF)

    with jax.named_scope("expert_sum_x"):
        cps = []
        for d in range(1, NX):
            to = lax.rem(x + d, NX)
            cps.append(send(rows(ms, to * ZR, ZR), rows(mr, x * ZR, ZR), msend.at[d - 1], mrecv.at[d - 1], at_x(d)))
        for cp in cps:
            cp.wait_recv()
        sends += cps
        mr[pl.ds(pl.multiple_of(x * ZR, 16), ZR), :] = ms[pl.ds(pl.multiple_of(x * ZR, 16), ZR), :]
        total = mr[0:ZR, :].astype(F32)
        for g in range(1, NX):
            total = total + mr[g * ZR : (g + 1) * ZR, :].astype(F32)
        total = total.astype(BF)
        p, s = iota((NZ * 16, ZR), 0), iota((NZ * 16, ZR), 1)
        wanted = (s == (p >> 4) * R + (p & 3)) & ((p & 3) < R)
        piece = jnp.zeros((NZ * 16, QW), F32)
        for q in range(4):
            piece = piece + mm(onehot(wanted & (((p >> 2) & 3) == q)), total[:, q * QW : (q + 1) * QW])
        zs[...] = piece.astype(BF)

    with jax.named_scope("expert_sum_z"):
        cps = []
        for d in [8] + [v for i in range(7, 0, -1) for v in (i, NZ - i)]:
            to = lax.rem(z + d, NZ)
            cps.append(send(rows(zs, to * 16, 16), rows(zr, z * 16, 16), zsend.at[d], zrecv.at[d], at_z(d)))
        for cp in cps:
            cp.wait_recv()
        sends += cps
        zr[pl.ds(pl.multiple_of(z * 16, 16), 16), :] = zs[pl.ds(pl.multiple_of(z * 16, 16), 16), :]
        total = hidden
        for g in range(NZ):
            total = total + zr[g * 16 : (g + 1) * 16, :].astype(F32)
        for q in range(4):
            out_ref[:, q * QW : (q + 1) * QW] = total[q * 4 : q * 4 + R, :].astype(BF)

    with jax.named_scope("drain"):
        for cp in a_cps + list(o_cps.values()) + c_cps + w_cps + list(h_cps.values()) + f_cps + sends:
            cp.wait_send()


def on_device(
    queries, new_key, new_value, cache_keys, cache_values, lengths, out_proj, residual, norm_gain,
    expert_ids, gate_weights, gate_proj, up_proj, down_proj,
):
    vmem = pl.BlockSpec(memory_space=pltpu.VMEM)
    dma = pltpu.SemaphoreType.DMA
    return pl.pallas_call(
        kernel,
        out_shape=jax.ShapeDtypeStruct((R, WD), BF),
        in_specs=[pl.BlockSpec(memory_space=pltpu.SMEM)] + [pl.BlockSpec(memory_space=pl.ANY)] * 13,
        out_specs=vmem,
        scratch_shapes=[
            pltpu.VMEM((R, KG), BF),
            pltpu.VMEM((R, HD), BF),
            pltpu.VMEM((R, HD), BF),
            pltpu.VMEM((R, SPAN, HD), BF),
            pltpu.VMEM((R, SPAN, HD), BF),
            pltpu.VMEM((KR, WD), BF),
            pltpu.VMEM((4 * R, WD), BF),
            pltpu.VMEM((WD,), BF),
            pltpu.VMEM((4, 4 * R), jnp.int32),
            pltpu.VMEM((4, 4 * R), BF),
            pltpu.VMEM((2 * FC, WD), BF),
            pltpu.VMEM((FC, WD), BF),
            pltpu.VMEM((16 * KR, WD // 2), BF),
            pltpu.VMEM((16 * 32, HD), BF),
            pltpu.VMEM((128, 16 * KR), BF),
            pltpu.VMEM((256, QW), BF),
            pltpu.VMEM((256, QW), BF),
            pltpu.VMEM((NX * 8, 2 * FC), F32),
            pltpu.VMEM((NX * NZ * 16, QW), BF),
            pltpu.VMEM((ROWS, WD), BF),
            pltpu.VMEM((ROWS, GW), BF),
            pltpu.VMEM((ROWS, GW), BF),
            pltpu.VMEM((ROWS, FC), BF),
            pltpu.VMEM((ROWS, WD), BF),
            pltpu.VMEM((ROWS, WD), BF),
            pltpu.VMEM((NZ * 16, QW), BF),
            pltpu.VMEM((NZ * 16, QW), BF),
            dma((13,)),
            dma((3,)), dma((3,)),
            dma((4,)), dma((4,)),
            dma((4,)), dma((4,)),
            dma((16,)), dma((16,)),
            dma((16,)), dma((16,)),
            dma((3,)), dma((3,)),
            dma((NZ,)), dma((NZ,)),
            dma((3 * NZ,)), dma((3 * NZ,)),
            dma((3,)), dma((3,)),
            dma((3,)), dma((3,)),
            dma((3,)), dma((3,)),
            dma((NZ,)), dma((NZ,)),
        ],
        compiler_params=pltpu.CompilerParams(
            collective_id=0, has_side_effects=True, vmem_limit_bytes=62 << 20
        ),
        name="decode_layer",
    )(
        lengths, queries, new_key, new_value, cache_keys, cache_values,
        out_proj.reshape(KR, WD), residual, norm_gain, expert_ids.T, gate_weights.T,
        gate_proj.reshape(F2, WD), up_proj.reshape(F2, WD), down_proj.reshape(F2, WD),
    )


def solution(mesh):
    placed = (
        P(("attn", "eslice"), "egrp"),
        P(("attn", "eslice"), "egrp"),
        P(("attn", "eslice"), "egrp"),
        P(("attn", "eslice"), None, "egrp"),
        P(("attn", "eslice"), None, "egrp"),
        P(("attn", "eslice")),
        P("egrp", "attn", "eslice"),
        P("attn", "eslice"),
        P("eslice"),
        P("attn", None),
        P("attn", None),
        P("egrp", "attn", "eslice"),
        P("egrp", "attn", "eslice"),
        P("egrp", "attn", "eslice"),
    )
    return jax.shard_map(
        on_device, mesh=mesh, in_specs=placed, out_specs=P(("attn", "egrp"), "eslice"), check_vma=False
    )
```

```python
import functools
import math

import jax
import jax.numpy as jnp
from jax import lax
from jax.experimental import pallas as pl
from jax.experimental.pallas import tpu as pltpu
from jax.sharding import PartitionSpec as P

D = 6144
HD = 128
HG = 6
SPAN = 512
R = 3
EPS = 1e-05
NZ, NX = 16, 4
WD = D // NX
QW = WD // 4
KR = 24
KG = 768
F2 = 336
FC = 2 * F2
ZR = NZ * R
NT, WT = 1, WD
GW = 2 * FC + 64
ROWS = NX * ZR
MESH = pl.DeviceIdType.MESH
BF = jnp.bfloat16
F32 = jnp.float32


def iota(shape, dim):
    return lax.broadcasted_iota(jnp.int32, shape, dim)


def onehot(cond):
    return jnp.where(cond, 1.0, 0.0).astype(BF)


def quotient(v, n):
    return (v * (65536 // n + 1)) >> 16


def mm(a, b):
    return jnp.dot(a, b, preferred_element_type=F32)


def mm_t(a, b):
    return lax.dot_general(a, b, (((1,), (1,)), ((), ())), preferred_element_type=F32)


def kernel(
    len_ref, q_hbm, nk_hbm, nv_hbm, ck_hbm, cv_hbm, op_hbm, res_hbm, gain_hbm, eid_hbm, gw_hbm,
    wg_ref, wu_ref, wd_ref,
    out_ref,
    qv, nkv, nvv, ckv, cvv, opv, resv, gainv, eidv, gwv, wgu, wdn, w2, at, a2, xs, xr, gs, hb, nm, gu, gr, ac, ms, mr, zs, zl, zc, zr,
    load_sem, wsend, wrecv, osend, orecv, csend, crecv, asend, arecv, xsend, xrecv, tsend, trecv,
    hsend, hrecv, fsend, frecv, gsend, grecv, bsend, brecv, msend, mrecv, zsend, zrecv,
):
    attn = lax.axis_index("attn")
    z, c = attn // 2, lax.rem(attn, 2)
    x, y = lax.axis_index("egrp"), lax.axis_index("eslice")

    def at_z(d):
        return (lax.rem(z + d + NZ, NZ) * 2 + c, x, y)

    def at_x(d):
        return (attn, lax.rem(x + d, NX), y)

    def at_y(d):
        return (attn, x, lax.rem(y + d, NX))

    quad, seat = z // 4, lax.rem(z, 4)

    def in_quad(s, dx, dy):
        return ((quad * 4 + s) * 2 + c, lax.rem(x + dx, NX), lax.rem(y + dy, NX))

    sibling = (z * 2 + 1 - c, x, y)
    others = [(k // 4, k % 4) for k in range(1, 16)]
    peers = [sibling]
    peers += [at_z(d) for d in range(-4, 5) if d]
    peers += [at_x(d) for d in range(1, NX)] + [at_y(d) for d in range(1, NX)]
    peers += [in_quad(lax.rem(seat + k, 4), m, 0) for k, m in others if k and m]
    peers += [in_quad(lax.rem(seat + k, 4), 0, m) for k, m in others if k and m]

    def send(src, dst, ssem, rsem, to):
        cp = pltpu.make_async_remote_copy(
            src_ref=src, dst_ref=dst, send_sem=ssem, recv_sem=rsem, device_id=to, device_id_type=MESH
        )
        cp.start()
        return cp

    def rows(ref, start, n):
        return ref.at[pl.ds(pl.multiple_of(start, 16), n)]

    barrier = pltpu.get_barrier_semaphore()
    for p in peers:
        pl.semaphore_signal(barrier, inc=1, device_id=p, device_id_type=MESH)

    def load(src, dst, sem):
        cp = pltpu.make_async_copy(src, dst, sem)
        cp.start()
        return cp

    l_q, l_nk, l_nv, l_ck, l_cv, l_op = [
        load(src, dst, load_sem.at[k])
        for k, (src, dst) in enumerate(
            ((q_hbm, qv), (nk_hbm, nkv), (nv_hbm, nvv), (ck_hbm, ckv), (cv_hbm, cvv), (op_hbm, opv))
        )
    ]
    l_rest = [
        load(src, dst, load_sem.at[k + 6])
        for k, (src, dst) in enumerate(((res_hbm, resv), (gain_hbm, gainv), (eid_hbm, eidv), (gw_hbm, gwv)))
    ]
    expert_weights = ((wg_ref, wgu, 0), (wu_ref, wgu, FC), (wd_ref, wdn, 0))
    loads = [
        load(src, rows(dst, base + c * F2, F2), load_sem.at[k + 10])
        for k, (src, dst, base) in enumerate(expert_weights)
    ]

    l_op.wait()
    own = opv[...].astype(F32)
    block = jnp.concatenate([own[:, : WD // 2], own[:, WD // 2 :]], axis=0).astype(BF)
    w2[pl.ds(pl.multiple_of((quad * 2 + c) * 2 * KR, 16), 2 * KR), :] = block

    sends = []
    with jax.named_scope("entry"):
        pl.semaphore_wait(barrier, len(peers))

    def block_of(d):
        return rows(w2, (lax.rem(quad - d + 8, 4) * 2 + c) * 2 * KR, 2 * KR)

    def pass_block(d, half, k, to):
        part = w2.at[
            pl.ds(pl.multiple_of((lax.rem(quad - d + 8, 4) * 2 + c) * 2 * KR, 16), 2 * KR), half * QW : (half + 1) * QW
        ]
        return send(part, part, osend.at[k], orecv.at[k], at_z(to))

    o_cps = [pass_block(0, 0, 0, 4), pass_block(0, 1, 1, -4), pass_block(0, 1, 2, 4), pass_block(0, 0, 3, -4)]
    c_cps = [send(block_of(0), block_of(0), csend.at[0], crecv.at[0], sibling)]

    with jax.named_scope("attention"):
        for cp in (l_q, l_nk, l_nv, l_ck, l_cv):
            cp.wait()
        qf = qv[...].astype(F32)
        pad2 = jnp.zeros((2, HD), F32)
        pieces = []
        for r in range(R):
            pieces += [qf[r : r + 1, h * HD : (h + 1) * HD] for h in range(HG)] + [pad2]
        q24 = jnp.concatenate(pieces, axis=0)
        q32 = jnp.concatenate([q24, jnp.zeros((8, HD), F32)], axis=0).astype(BF)
        nk24 = jnp.concatenate([jnp.broadcast_to(nkv[r : r + 1, :].astype(F32), (8, HD)) for r in range(R)], 0)
        nv24 = jnp.concatenate([jnp.broadcast_to(nvv[r : r + 1, :].astype(F32), (8, HD)) for r in range(R)], 0)
        len24 = jnp.concatenate([jnp.full((8, 1), len_ref[r], jnp.int32) for r in range(R)], 0)
        scale = 1.0 / math.sqrt(HD)
        scores = jnp.concatenate([mm_t(q32, ckv[r])[r * 8 : (r + 1) * 8] for r in range(R)], 0) * scale
        self_score = jnp.sum(q24 * nk24, axis=1, keepdims=True) * scale
        live = iota((R * 8, SPAN), 1) < len24
        scores = jnp.where(live, scores, -1e30)
        highest = jnp.maximum(jnp.max(scores, axis=1, keepdims=True), self_score)
        expos = jnp.where(live, jnp.exp(scores - highest), 0.0)
        own_exp = jnp.exp(self_score - highest)
        totals = jnp.sum(expos, axis=1, keepdims=True) + own_exp
        weights = jnp.concatenate([expos / totals, jnp.zeros((8, SPAN), F32)], axis=0).astype(BF)
        own_weight = (own_exp / totals).astype(BF).astype(F32)
        summed = jnp.concatenate([mm(weights, cvv[r])[r * 8 : (r + 1) * 8] for r in range(R)], 0)
        summed = summed + own_weight * nv24
        at[pl.ds(pl.multiple_of((seat * 4 + y) * 32, 16), 32), :] = jnp.concatenate(
            [summed, jnp.zeros((8, HD), F32)], axis=0
        ).astype(BF)

    mine = rows(at, (seat * 4 + y) * 32, 32)
    a_cps = [
        send(mine, mine, asend.at[k * 4 + m], arecv.at[k * 4 + m], in_quad(lax.rem(seat + k, 4), 0, m))
        for k, m in others
    ]
    w_cps = []
    for k, (src, dst, base) in enumerate(expert_weights):
        w_cps.append(send(src, rows(dst, base + c * F2, F2), wsend.at[k], wrecv.at[k], sibling))

    for cp in l_rest:
        cp.wait()
    row16, lane16 = iota((16, 4 * R), 0), iota((16, 4 * R), 1)
    part = row16 & 3
    wanted = (lane16 == x * R + part) & (part < R)
    res16 = jnp.zeros((16, QW), F32)
    for q in range(4):
        res16 = res16 + mm(onehot(wanted & ((row16 >> 2) == q)), resv[:, q * QW : (q + 1) * QW])
    gain_row = gainv[...].reshape(1, WD)
    gain16 = jnp.concatenate(
        [jnp.broadcast_to(gain_row[:, q * QW : (q + 1) * QW].astype(F32), (4, QW)) for q in range(4)], 0
    )
    gwf = gwv[...].astype(F32)
    expert = iota((128, 4 * R), 0)
    shares = jnp.zeros((128, 4 * R), F32)
    for k in range(4):
        shares = shares + jnp.where(expert == eidv[k : k + 1, :], gwf[k : k + 1, :], 0.0)
    share16 = mm_t(onehot(lane16 == x * R + (row16 >> 2)), shares.astype(BF))

    with jax.named_scope("projection_relay"):
        o_cps[0].wait_recv()
        o_cps.append(pass_block(1, 0, 4, 4))
        o_cps[1].wait_recv()
        o_cps.append(pass_block(-1, 1, 5, -4))

    with jax.named_scope("attended_gather"):
        for cp in a_cps:
            cp.wait_recv()
        p, s = iota((HG * 64, 512), 0), iota((HG * 64, 512), 1)
        pick = onehot(s == ((p & 63) >> 2) * 32 + (p & 3) * 8 + (p >> 6))
        heads = mm(pick, at[...]).astype(BF)
        a64 = jnp.concatenate([heads[h * 64 : (h + 1) * 64] for h in range(HG)], axis=1)
        j = iota((1, 16 * KR), 1)
        slot = quotient(j, 2 * KR)
        rem = j - slot * 2 * KR
        later = rem >= KR
        source = (((slot >> 1) * 4 + seat) * 2 + (slot & 1)) * KR + jnp.where(later, rem - KR, rem)
        wide = mm(a64, onehot(iota((KG, 16 * KR), 0) == source))
        a2[...] = jnp.concatenate([jnp.where(later, 0.0, wide), jnp.where(later, wide, 0.0)], axis=0).astype(BF)

    with jax.named_scope("projection_gather"):
        for d, first, second in ((1, 0, 2), (-1, 1, 3), (2, 4, 5)):
            if d == 2:
                o_cps[first].wait_recv()
            o_cps[second].wait_recv()
            c_cps.append(send(block_of(d), block_of(d), csend.at[d % 4], crecv.at[d % 4], sibling))

    with jax.named_scope("gain_sums"):
        for cp in loads:
            cp.wait()
        for cp in w_cps:
            cp.wait_recv()
        gains = jnp.broadcast_to(gain_row, (16, WD))
        for lo, hi in ((0, 512), (512, 1024), (1024, 2 * FC)):
            gs[pl.ds(pl.multiple_of(y * 8, 8), 8), lo:hi] = mm_t(gains, wgu[lo:hi, :])[0:8]
        mine = gs.at[pl.ds(pl.multiple_of(y * 8, 8), 8)]
        g_cps = [send(mine, mine, tsend.at[d - 1], trecv.at[d - 1], at_y(d)) for d in range(1, NX)]

    with jax.named_scope("projection"):
        for cp in c_cps:
            cp.wait_recv()
        mixed = mm(a2[...], w2[...]).astype(BF)
        p, s = iota((256, 128), 0), iota((256, 128), 1)
        source = (((p >> 3) & 1) << 6) + ((p >> 4) << 2) + (p & 3)
        odd = ((p >> 2) & 1) == 1
        xs[...] = (
            mm(onehot((s == source) & ~odd), mixed[:, :QW]) + mm(onehot((s == source) & odd), mixed[:, QW:])
        ).astype(BF)

    with jax.named_scope("projection_terms"):
        slot = (seat * 4 + x) * 16
        cps = []
        for k, m in others:
            to = lax.rem(seat + k, 4)
            n = k * 4 + m
            cps.append(
                send(
                    rows(xs, (to * 4 + lax.rem(x + m, NX)) * 16, 16), rows(xr, slot, 16),
                    xsend.at[n], xrecv.at[n], in_quad(to, m, 0),
                )
            )
        for cp in cps:
            cp.wait_recv()
        sends += cps
        xr[pl.ds(pl.multiple_of(slot, 16), 16), :] = xs[pl.ds(pl.multiple_of(slot, 16), 16), :]
        hidden = res16
        for g in range(16):
            hidden = hidden + xr[g * 16 : (g + 1) * 16, :].astype(F32)
        hidden = hidden.astype(BF).astype(F32)

    with jax.named_scope("center_slice"):
        def per_request(v):
            v = jnp.sum(v, axis=1, keepdims=True)
            v = v[0:8] + v[8:16]
            v = v[0:4] + v[4:8]
            return jnp.concatenate([v] * 4, axis=0)

        def halves(v):
            high = v.astype(BF).astype(F32)
            return high, v - high

        mean = (per_request(hidden) / WD).astype(BF).astype(F32)
        inside = (iota((16, QW), 0) & 3) < R
        near = jnp.where(inside, hidden - mean, 0.0)
        notes = (mean,) + halves(per_request(near)) + halves(per_request(near * near))
        lane = iota((16, 128), 1)
        row = iota((16, 128), 0)
        extra = jnp.where(lane < 8, share16, 0.0)
        for j, note in enumerate(notes):
            by_request = jnp.concatenate([jnp.broadcast_to(note[i : i + 1], (4, 1)) for i in range(4)], axis=0)
            extra = extra + jnp.where(lane == 8 + j, by_request, 0.0)
        extra = jnp.where((row & 3) == R, extra, 0.0)
        extra = jnp.concatenate([extra, jnp.zeros((16, QW - 128), F32)], axis=1)
        hb[pl.ds(pl.multiple_of((x * NZ + z) * 16, 16), 16), :] = (near * gain16 + extra).astype(BF)

    with jax.named_scope("token_gather"):
        f_cps = []

        def over_x(d):
            blk = rows(hb, (x * NZ + lax.rem(z - d + NZ, NZ)) * 16, 16)
            for k in (2, 1, 3):
                n = (k - 1) * NZ + d % NZ
                f_cps.append(send(blk, blk, fsend.at[n], frecv.at[n], at_x(k)))

        blk = rows(hb, (x * NZ + z) * 16, 16)
        h_cps = {}
        for d in (4, -4, 3, -3, 2, -2, 1, -1):
            h_cps[d] = send(blk, blk, hsend.at[d % NZ], hrecv.at[d % NZ], at_z(d))
        over_x(0)
        for sign in (1, -1):
            h_cps[sign * 4].wait_recv()
            blk = rows(hb, (x * NZ + lax.rem(z - sign * 4 + NZ, NZ)) * 16, 16)
            for s in (4, 3, 2, 1) if sign > 0 else (3, 2, 1):
                n = sign * (4 + s)
                h_cps[n] = send(blk, blk, hsend.at[n % NZ], hrecv.at[n % NZ], at_z(sign * s))
        for d in (4, -4):
            over_x(d)
        for d in (1, -1, 2, -2, 3, -3, 5, -5, 6, -6, 7, -7, 8):
            h_cps[d].wait_recv()
            over_x(d)
        for cp in f_cps:
            cp.wait_recv()

    with jax.named_scope("compact"):
        p, s = iota((4 * ZR, NZ * 16), 0), iota((4 * ZR, NZ * 16), 1)
        quarter = quotient(p, ZR)
        m = p - quarter * ZR
        who = quotient(m, R)
        pick = onehot(s == who * 16 + quarter * 4 + (m - who * R))
        for g in range(NX):
            got = mm(pick, hb[g * NZ * 16 : (g + 1) * NZ * 16, :]).astype(BF)
            for q in range(4):
                nm[g * ZR : (g + 1) * ZR, q * QW : (q + 1) * QW] = got[q * ZR : (q + 1) * ZR]
        p, s = iota((ZR, NZ * 16), 0), iota((ZR, NZ * 16), 1)
        who = quotient(p, R)
        pick = onehot(s == who * 16 + (p - who * R) * 4 + R)
        for g in range(NX):
            gu[g * ZR : (g + 1) * ZR, 2 * FC : 2 * FC + 16] = mm(
                pick, hb[g * NZ * 16 : (g + 1) * NZ * 16, 0:128]
            )[:, 0:16].astype(BF)

    with jax.named_scope("gate_up"):
        tokens = nm[...]
        for lo, hi in ((0, 512), (512, 1024), (1024, 2 * FC)):
            gu[:, lo:hi] = mm_t(tokens, wgu[lo:hi, :]).astype(BF)

    with jax.named_scope("gate_up_terms"):
        cps = []
        for d in range(1, NX):
            to = lax.rem(y + d, NX)
            cps.append(send(rows(gu, to * ZR, ZR), rows(gr, y * ZR, ZR), gsend.at[d - 1], grecv.at[d - 1], at_y(d)))
        for cp in cps:
            cp.wait_recv()
        sends += cps + g_cps
        gr[pl.ds(pl.multiple_of(y * ZR, 16), ZR), :] = gu[pl.ds(pl.multiple_of(y * ZR, 16), ZR), :]

    with jax.named_scope("activation"):
        total = gr[0:ZR, :].astype(F32)
        for g in range(1, NX):
            total = total + gr[g * ZR : (g + 1) * ZR, :].astype(F32)
        for cp in g_cps:
            cp.wait_recv()
        notes = [gr[g * ZR : (g + 1) * ZR, 2 * FC : 2 * FC + 16].astype(F32) for g in range(NX)]
        means = [n[:, 8:9] for n in notes]
        sums = [n[:, 9:10] + n[:, 10:11] for n in notes]
        squares = [n[:, 11:12] + n[:, 12:13] for n in notes]
        center = sum(s + WD * m for s, m in zip(sums, means)) / D
        apart = [m - center for m in means]
        spread = sum(q + 2.0 * a * s + WD * a * a for q, a, s in zip(squares, apart, sums)) / D
        whole = total[:, : 2 * FC]
        for g in range(NX):
            whole = whole + apart[g] * gs[g * 8 : g * 8 + 1, :]
        whole = whole * lax.rsqrt(spread + EPS)
        lane = iota((ZR, 16), 1)
        share0 = jnp.sum(jnp.where(lane == x * 2, notes[0], 0.0), axis=1, keepdims=True)
        share1 = jnp.sum(jnp.where(lane == x * 2 + 1, notes[0], 0.0), axis=1, keepdims=True)
        gate, up = whole[:, :FC], whole[:, FC:]
        unit = iota((ZR, FC), 1)
        unit = jnp.where(unit >= F2, unit - F2, unit)
        share = jnp.where(unit >= F2 // 2, share1, share0)
        mine = rows(ac, y * ZR, ZR)
        ac[pl.ds(pl.multiple_of(y * ZR, 16), ZR), :] = (gate / (1.0 + jnp.exp(-gate)) * up * share).astype(BF)

    with jax.named_scope("activation_gather"):
        cps = [send(mine, mine, bsend.at[d - 1], brecv.at[d - 1], at_y(d)) for d in range(1, NX)]
        for cp in cps:
            cp.wait_recv()
        sends += cps

    with jax.named_scope("down"):
        act = ac[...]
        m_cps = []
        for t in range(NT):
            cols = slice(t * WT, (t + 1) * WT)
            for lo in range(0, WT, 512):
                ms[:, lo : lo + 512] = mm(act, wdn[:, lo : lo + 512]).astype(BF)
            for d in range(1, NX):
                to = lax.rem(x + d, NX)
                n = t * 3 + d - 1
                m_cps.append(
                    send(
                        ms.at[pl.ds(pl.multiple_of(to * ZR, 16), ZR), cols],
                        mr.at[pl.ds(pl.multiple_of(x * ZR, 16), ZR), cols],
                        msend.at[n], mrecv.at[n], at_x(d),
                    )
                )

    p, s = iota((NZ * 16, ZR), 0), iota((NZ * 16, ZR), 1)
    wanted = (s == (p >> 4) * R + (p & 3)) & ((p & 3) < R)
    picks = [onehot(wanted & (((p >> 2) & 3) == q)) for q in range(4)]
    z_cps = {}

    def piece(t, d):
        return pl.ds(pl.multiple_of(t * NZ * 16 + lax.rem(z + d + NZ, NZ) * 16, 16), 16)

    def slot(t, n, k):
        return slice((t * n + k) * 16, (t * n + k + 1) * 16)

    def sum_over_x(t):
        cols = slice(t * WT, (t + 1) * WT)
        for cp in m_cps[t * 3 : t * 3 + 3]:
            cp.wait_recv()
        here = pl.ds(pl.multiple_of(x * ZR, 16), ZR)
        mr[here, cols] = ms[here, cols]
        total = mr[0:ZR, cols].astype(F32)
        for g in range(1, NX):
            total = total + mr[g * ZR : (g + 1) * ZR, cols].astype(F32)
        total = total.astype(BF)
        tiles = jnp.zeros((NZ * 16, WT // 4), F32)
        for q in range(4):
            tiles = tiles + mm(picks[q], total[:, q * WT // 4 : (q + 1) * WT // 4])
        zs[t * NZ * 16 : (t + 1) * NZ * 16, :] = tiles.astype(BF)
        for k, d in ((3, 8), (2, 7), (6, -7), (1, 6), (5, -6), (0, 5), (4, -5)):
            to = d - 4 if d > 0 else d + 4
            n = t * 15 + k
            z_cps[n] = send(zs.at[piece(t, d)], zl.at[slot(t, 7, k)], zsend.at[n], zrecv.at[n], at_z(to))
        for k, d in ((2, 3), (5, -3), (1, 2), (4, -2), (0, 1), (3, -1)):
            n = t * 15 + 7 + k
            z_cps[n] = send(zs.at[piece(t, d)], zr.at[slot(t, 8, k)], zsend.at[n], zrecv.at[n], at_z(d))

    def relay(t):
        for way, d, ks in ((0, 4, (0, 1, 2, 3)), (1, -4, (4, 5, 6))):
            total = zs[piece(t, d), :].astype(F32)
            for k in ks:
                z_cps[t * 15 + k].wait_recv()
                total = total + zl[slot(t, 7, k), :].astype(F32)
            zc[slot(t, 2, way), :] = total.astype(BF)
            n = t * 15 + 13 + way
            z_cps[n] = send(zc.at[slot(t, 2, way)], zr.at[slot(t, 8, 6 + way)], zsend.at[n], zrecv.at[n], at_z(d))

    with jax.named_scope("expert_sums"):
        sum_over_x(0)
        relay(0)
    with jax.named_scope("last_sum"):
        for t in range(NT):
            total = zs[piece(t, 0), :].astype(F32)
            for k in range(8):
                z_cps[t * 15 + 7 + k].wait_recv()
                total = total + zr[slot(t, 8, k), :].astype(F32)
            for q in range(4):
                out_ref[:, q * QW : (q + 1) * QW] = (hidden + total)[q * 4 : q * 4 + R].astype(BF)

    with jax.named_scope("drain"):
        for cp in a_cps + o_cps + c_cps + w_cps + m_cps + list(z_cps.values()) + list(h_cps.values()) + f_cps + sends:
            cp.wait_send()


def on_device(
    queries, new_key, new_value, cache_keys, cache_values, lengths, out_proj, residual, norm_gain,
    expert_ids, gate_weights, gate_proj, up_proj, down_proj,
):
    vmem = pl.BlockSpec(memory_space=pltpu.VMEM)
    dma = pltpu.SemaphoreType.DMA
    return pl.pallas_call(
        kernel,
        out_shape=jax.ShapeDtypeStruct((R, WD), BF),
        in_specs=[pl.BlockSpec(memory_space=pltpu.SMEM)] + [pl.BlockSpec(memory_space=pl.ANY)] * 13,
        out_specs=vmem,
        scratch_shapes=[
            pltpu.VMEM((R, KG), BF),
            pltpu.VMEM((R, HD), BF),
            pltpu.VMEM((R, HD), BF),
            pltpu.VMEM((R, SPAN, HD), BF),
            pltpu.VMEM((R, SPAN, HD), BF),
            pltpu.VMEM((KR, WD), BF),
            pltpu.VMEM((4 * R, WD), BF),
            pltpu.VMEM((WD,), BF),
            pltpu.VMEM((4, 4 * R), jnp.int32),
            pltpu.VMEM((4, 4 * R), BF),
            pltpu.VMEM((2 * FC, WD), BF),
            pltpu.VMEM((FC, WD), BF),
            pltpu.VMEM((16 * KR, WD // 2), BF),
            pltpu.VMEM((16 * 32, HD), BF),
            pltpu.VMEM((128, 16 * KR), BF),
            pltpu.VMEM((256, QW), BF),
            pltpu.VMEM((256, QW), BF),
            pltpu.VMEM((NX * 8, 2 * FC), F32),
            pltpu.VMEM((NX * NZ * 16, QW), BF),
            pltpu.VMEM((ROWS, WD), BF),
            pltpu.VMEM((ROWS, GW), BF),
            pltpu.VMEM((ROWS, GW), BF),
            pltpu.VMEM((ROWS, FC), BF),
            pltpu.VMEM((ROWS, WD), BF),
            pltpu.VMEM((ROWS, WD), BF),
            pltpu.VMEM((NT * NZ * 16, WT // 4), BF),
            pltpu.VMEM((NT * 7 * 16, WT // 4), BF),
            pltpu.VMEM((NT * 2 * 16, WT // 4), BF),
            pltpu.VMEM((NT * 8 * 16, WT // 4), BF),
            dma((13,)),
            dma((3,)), dma((3,)),
            dma((6,)), dma((6,)),
            dma((4,)), dma((4,)),
            dma((16,)), dma((16,)),
            dma((16,)), dma((16,)),
            dma((3,)), dma((3,)),
            dma((NZ,)), dma((NZ,)),
            dma((3 * NZ,)), dma((3 * NZ,)),
            dma((3,)), dma((3,)),
            dma((3,)), dma((3,)),
            dma((3 * NT,)), dma((3 * NT,)),
            dma((15 * NT,)), dma((15 * NT,)),
        ],
        compiler_params=pltpu.CompilerParams(
            collective_id=0, has_side_effects=True, vmem_limit_bytes=62 << 20
        ),
        name="decode_layer",
    )(
        lengths, queries, new_key, new_value, cache_keys, cache_values,
        out_proj.reshape(KR, WD), residual, norm_gain, expert_ids.T, gate_weights.T,
        gate_proj.reshape(F2, WD), up_proj.reshape(F2, WD), down_proj.reshape(F2, WD),
    )


def solution(mesh):
    placed = (
        P(("attn", "eslice"), "egrp"),
        P(("attn", "eslice"), "egrp"),
        P(("attn", "eslice"), "egrp"),
        P(("attn", "eslice"), None, "egrp"),
        P(("attn", "eslice"), None, "egrp"),
        P(("attn", "eslice")),
        P("egrp", "attn", "eslice"),
        P("attn", "eslice"),
        P("eslice"),
        P("attn", None),
        P("attn", None),
        P("egrp", "attn", "eslice"),
        P("egrp", "attn", "eslice"),
        P("egrp", "attn", "eslice"),
    )
    return jax.shard_map(
        on_device, mesh=mesh, in_specs=placed, out_specs=P(("attn", "egrp"), "eslice"), check_vma=False
    )
```

```python
import functools
import math

import jax
import jax.numpy as jnp
from jax import lax
from jax.experimental import pallas as pl
from jax.experimental.pallas import tpu as pltpu
from jax.sharding import PartitionSpec as P

D = 6144
HD = 128
HG = 6
SPAN = 512
R = 3
EPS = 1e-05
NZ, NX = 16, 4
WD = D // NX
QW = WD // 4
KR = 24
KG = 768
F2 = 336
FC = 2 * F2
ZR = NZ * R
NT, WT = 1, WD
GW = 768
ROWS = NX * ZR
MESH = pl.DeviceIdType.MESH
BF = jnp.bfloat16
F32 = jnp.float32


def iota(shape, dim):
    return lax.broadcasted_iota(jnp.int32, shape, dim)


def onehot(cond):
    return jnp.where(cond, 1.0, 0.0).astype(BF)


def quotient(v, n):
    return (v * (65536 // n + 1)) >> 16


def mm(a, b):
    return jnp.dot(a, b, preferred_element_type=F32)


def mm_t(a, b):
    return lax.dot_general(a, b, (((1,), (1,)), ((), ())), preferred_element_type=F32)


def kernel(
    len_ref, q_hbm, nk_hbm, nv_hbm, ck_hbm, cv_hbm, op_hbm, res_hbm, gain_hbm, eid_hbm, gw_hbm,
    wg_ref, wu_ref, wd_ref,
    out_ref,
    qv, nkv, nvv, ckv, cvv, opv, resv, gainv, eidv, gwv, wgu, wdn, w2, at, a2, xs, xr, gs, hb, nm, gu, gr, ac, ms, mr, zs, zl, zc, zr,
    load_sem, wsend, wrecv, osend, orecv, csend, crecv, asend, arecv, xsend, xrecv, tsend, trecv,
    hsend, hrecv, fsend, frecv, gsend, grecv, bsend, brecv, msend, mrecv, zsend, zrecv,
):
    attn = lax.axis_index("attn")
    z, c = attn // 2, lax.rem(attn, 2)
    x, y = lax.axis_index("egrp"), lax.axis_index("eslice")

    def at_z(d):
        return (lax.rem(z + d + NZ, NZ) * 2 + c, x, y)

    def at_x(d):
        return (attn, lax.rem(x + d, NX), y)

    def at_y(d):
        return (attn, x, lax.rem(y + d, NX))

    quad, seat = z // 4, lax.rem(z, 4)

    def in_quad(s, dx, dy):
        return ((quad * 4 + s) * 2 + c, lax.rem(x + dx, NX), lax.rem(y + dy, NX))

    sibling = (z * 2 + 1 - c, x, y)
    others = [(k // 4, k % 4) for k in range(1, 16)]
    peers = [sibling]
    peers += [at_z(d) for d in range(-4, 5) if d]
    peers += [at_x(d) for d in range(1, NX)] + [at_y(d) for d in range(1, NX)]
    peers += [in_quad(lax.rem(seat + k, 4), m, 0) for k, m in others if k and m]
    peers += [in_quad(lax.rem(seat + k, 4), 0, m) for k, m in others if k and m]

    def send(src, dst, ssem, rsem, to):
        cp = pltpu.make_async_remote_copy(
            src_ref=src, dst_ref=dst, send_sem=ssem, recv_sem=rsem, device_id=to, device_id_type=MESH
        )
        cp.start()
        return cp

    def rows(ref, start, n):
        return ref.at[pl.ds(pl.multiple_of(start, 16), n)]

    barrier = pltpu.get_barrier_semaphore()
    for p in peers:
        pl.semaphore_signal(barrier, inc=1, device_id=p, device_id_type=MESH)

    def load(src, dst, sem):
        cp = pltpu.make_async_copy(src, dst, sem)
        cp.start()
        return cp

    l_q, l_nk, l_nv, l_ck, l_cv, l_op = [
        load(src, dst, load_sem.at[k])
        for k, (src, dst) in enumerate(
            ((q_hbm, qv), (nk_hbm, nkv), (nv_hbm, nvv), (ck_hbm, ckv), (cv_hbm, cvv), (op_hbm, opv))
        )
    ]
    l_rest = [
        load(src, dst, load_sem.at[k + 6])
        for k, (src, dst) in enumerate(((res_hbm, resv), (gain_hbm, gainv), (eid_hbm, eidv), (gw_hbm, gwv)))
    ]
    expert_weights = ((wg_ref, wgu, c * FC), (wu_ref, wgu, c * FC + F2), (wd_ref, wdn, c * F2))
    loads = [
        load(src, rows(dst, base, F2), load_sem.at[k + 10])
        for k, (src, dst, base) in enumerate(expert_weights)
    ]

    l_op.wait()
    own = opv[...].astype(F32)
    block = jnp.concatenate([own[:, : WD // 2], own[:, WD // 2 :]], axis=0).astype(BF)
    w2[pl.ds(pl.multiple_of((quad * 2 + c) * 2 * KR, 16), 2 * KR), :] = block

    sends = []
    with jax.named_scope("entry"):
        pl.semaphore_wait(barrier, len(peers))

    def block_of(d):
        return rows(w2, (lax.rem(quad - d + 8, 4) * 2 + c) * 2 * KR, 2 * KR)

    def pass_block(d, half, k, to):
        part = w2.at[
            pl.ds(pl.multiple_of((lax.rem(quad - d + 8, 4) * 2 + c) * 2 * KR, 16), 2 * KR), half * QW : (half + 1) * QW
        ]
        return send(part, part, osend.at[k], orecv.at[k], at_z(to))

    o_cps = [pass_block(0, 0, 0, 4), pass_block(0, 1, 1, -4), pass_block(0, 1, 2, 4), pass_block(0, 0, 3, -4)]
    c_cps = [send(block_of(0), block_of(0), csend.at[0], crecv.at[0], sibling)]

    with jax.named_scope("attention"):
        for cp in (l_q, l_nk, l_nv, l_ck, l_cv):
            cp.wait()
        qf = qv[...].astype(F32)
        pad2 = jnp.zeros((2, HD), F32)
        pieces = []
        for r in range(R):
            pieces += [qf[r : r + 1, h * HD : (h + 1) * HD] for h in range(HG)] + [pad2]
        q24 = jnp.concatenate(pieces, axis=0)
        q32 = jnp.concatenate([q24, jnp.zeros((8, HD), F32)], axis=0).astype(BF)
        nk24 = jnp.concatenate([jnp.broadcast_to(nkv[r : r + 1, :].astype(F32), (8, HD)) for r in range(R)], 0)
        nv24 = jnp.concatenate([jnp.broadcast_to(nvv[r : r + 1, :].astype(F32), (8, HD)) for r in range(R)], 0)
        len24 = jnp.concatenate([jnp.full((8, 1), len_ref[r], jnp.int32) for r in range(R)], 0)
        scale = 1.0 / math.sqrt(HD)
        scores = jnp.concatenate([mm_t(q32, ckv[r])[r * 8 : (r + 1) * 8] for r in range(R)], 0) * scale
        self_score = jnp.sum(q24 * nk24, axis=1, keepdims=True) * scale
        live = iota((R * 8, SPAN), 1) < len24
        scores = jnp.where(live, scores, -1e30)
        highest = jnp.maximum(jnp.max(scores, axis=1, keepdims=True), self_score)
        expos = jnp.where(live, jnp.exp(scores - highest), 0.0)
        own_exp = jnp.exp(self_score - highest)
        totals = jnp.sum(expos, axis=1, keepdims=True) + own_exp
        weights = jnp.concatenate([expos / totals, jnp.zeros((8, SPAN), F32)], axis=0).astype(BF)
        own_weight = (own_exp / totals).astype(BF).astype(F32)
        summed = jnp.concatenate([mm(weights, cvv[r])[r * 8 : (r + 1) * 8] for r in range(R)], 0)
        summed = summed + own_weight * nv24
        at[pl.ds(pl.multiple_of((seat * 4 + y) * 32, 16), 32), :] = jnp.concatenate(
            [summed, jnp.zeros((8, HD), F32)], axis=0
        ).astype(BF)

    mine = rows(at, (seat * 4 + y) * 32, 32)
    a_cps = [
        send(mine, mine, asend.at[k * 4 + m], arecv.at[k * 4 + m], in_quad(lax.rem(seat + k, 4), 0, m))
        for k, m in others
    ]
    w_cps = []
    for k, (src, dst, base) in enumerate(expert_weights):
        w_cps.append(send(src, rows(dst, base, F2), wsend.at[k], wrecv.at[k], sibling))

    for cp in l_rest:
        cp.wait()
    row16, lane16 = iota((16, 4 * R), 0), iota((16, 4 * R), 1)
    part = row16 & 3
    wanted = (lane16 == x * R + part) & (part < R)
    res16 = jnp.zeros((16, QW), F32)
    for q in range(4):
        res16 = res16 + mm(onehot(wanted & ((row16 >> 2) == q)), resv[:, q * QW : (q + 1) * QW])
    gain_row = gainv[...].reshape(1, WD)
    gain16 = jnp.concatenate(
        [jnp.broadcast_to(gain_row[:, q * QW : (q + 1) * QW].astype(F32), (4, QW)) for q in range(4)], 0
    )
    gwf = gwv[...].astype(F32)
    expert = iota((128, 4 * R), 0)
    shares = jnp.zeros((128, 4 * R), F32)
    for k in range(4):
        shares = shares + jnp.where(expert == eidv[k : k + 1, :], gwf[k : k + 1, :], 0.0)
    share16 = mm_t(onehot(lane16 == x * R + (row16 >> 2)), shares.astype(BF))

    with jax.named_scope("projection_relay"):
        o_cps[0].wait_recv()
        o_cps.append(pass_block(1, 0, 4, 4))
        o_cps[1].wait_recv()
        o_cps.append(pass_block(-1, 1, 5, -4))

    with jax.named_scope("attended_gather"):
        for cp in a_cps:
            cp.wait_recv()
        p, s = iota((HG * 64, 512), 0), iota((HG * 64, 512), 1)
        pick = onehot(s == ((p & 63) >> 2) * 32 + (p & 3) * 8 + (p >> 6))
        heads = mm(pick, at[...]).astype(BF)
        a64 = jnp.concatenate([heads[h * 64 : (h + 1) * 64] for h in range(HG)], axis=1)
        j = iota((1, 16 * KR), 1)
        slot = quotient(j, 2 * KR)
        rem = j - slot * 2 * KR
        later = rem >= KR
        source = (((slot >> 1) * 4 + seat) * 2 + (slot & 1)) * KR + jnp.where(later, rem - KR, rem)
        wide = mm(a64, onehot(iota((KG, 16 * KR), 0) == source))
        a2[...] = jnp.concatenate([jnp.where(later, 0.0, wide), jnp.where(later, wide, 0.0)], axis=0).astype(BF)

    with jax.named_scope("projection_gather"):
        for d, first, second in ((1, 0, 2), (-1, 1, 3), (2, 4, 5)):
            if d == 2:
                o_cps[first].wait_recv()
            o_cps[second].wait_recv()
            c_cps.append(send(block_of(d), block_of(d), csend.at[d % 4], crecv.at[d % 4], sibling))

    with jax.named_scope("gain_sums"):
        for cp in loads:
            cp.wait()
        for cp in w_cps:
            cp.wait_recv()
        gains = jnp.broadcast_to(gain_row, (16, WD))
        for lo, hi in ((0, 512), (512, 1024), (1024, 2 * FC)):
            gs[pl.ds(pl.multiple_of(y * 8, 8), 8), lo:hi] = mm_t(gains, wgu[lo:hi, :])[0:8]
        mine = gs.at[pl.ds(pl.multiple_of(y * 8, 8), 8)]
        g_cps = [send(mine, mine, tsend.at[d - 1], trecv.at[d - 1], at_y(d)) for d in range(1, NX)]

    with jax.named_scope("projection"):
        for cp in c_cps:
            cp.wait_recv()
        mixed = mm(a2[...], w2[...]).astype(BF)
        p, s = iota((256, 128), 0), iota((256, 128), 1)
        source = (((p >> 3) & 1) << 6) + ((p >> 4) << 2) + (p & 3)
        odd = ((p >> 2) & 1) == 1
        xs[...] = (
            mm(onehot((s == source) & ~odd), mixed[:, :QW]) + mm(onehot((s == source) & odd), mixed[:, QW:])
        ).astype(BF)

    with jax.named_scope("projection_terms"):
        slot = (seat * 4 + x) * 16
        cps = []
        for k, m in others:
            to = lax.rem(seat + k, 4)
            n = k * 4 + m
            cps.append(
                send(
                    rows(xs, (to * 4 + lax.rem(x + m, NX)) * 16, 16), rows(xr, slot, 16),
                    xsend.at[n], xrecv.at[n], in_quad(to, m, 0),
                )
            )
        for cp in cps:
            cp.wait_recv()
        sends += cps
        xr[pl.ds(pl.multiple_of(slot, 16), 16), :] = xs[pl.ds(pl.multiple_of(slot, 16), 16), :]
        hidden = res16
        for g in range(16):
            hidden = hidden + xr[g * 16 : (g + 1) * 16, :].astype(F32)
        hidden = hidden.astype(BF).astype(F32)

    with jax.named_scope("center_slice"):
        def per_request(v):
            v = jnp.sum(v, axis=1, keepdims=True)
            v = v[0:8] + v[8:16]
            v = v[0:4] + v[4:8]
            return jnp.concatenate([v] * 4, axis=0)

        def halves(v):
            high = v.astype(BF).astype(F32)
            return high, v - high

        mean = (per_request(hidden) / WD).astype(BF).astype(F32)
        inside = (iota((16, QW), 0) & 3) < R
        near = jnp.where(inside, hidden - mean, 0.0)
        notes = (mean,) + halves(per_request(near)) + halves(per_request(near * near))
        lane = iota((16, 128), 1)
        row = iota((16, 128), 0)
        extra = jnp.where(lane < 8, share16, 0.0)
        for j, note in enumerate(notes):
            by_request = jnp.concatenate([jnp.broadcast_to(note[i : i + 1], (4, 1)) for i in range(4)], axis=0)
            extra = extra + jnp.where(lane == 8 + j, by_request, 0.0)
        extra = jnp.where((row & 3) == R, extra, 0.0)
        extra = jnp.concatenate([extra, jnp.zeros((16, QW - 128), F32)], axis=1)
        hb[pl.ds(pl.multiple_of((x * NZ + z) * 16, 16), 16), :] = (near * gain16 + extra).astype(BF)

    with jax.named_scope("token_gather"):
        f_cps = []

        def over_x(d):
            blk = rows(hb, (x * NZ + lax.rem(z - d + NZ, NZ)) * 16, 16)
            for k in (2, 1, 3):
                n = (k - 1) * NZ + d % NZ
                f_cps.append(send(blk, blk, fsend.at[n], frecv.at[n], at_x(k)))

        blk = rows(hb, (x * NZ + z) * 16, 16)
        h_cps = {}
        for d in (4, -4, 3, -3, 2, -2, 1, -1):
            h_cps[d] = send(blk, blk, hsend.at[d % NZ], hrecv.at[d % NZ], at_z(d))
        over_x(0)
        for sign in (1, -1):
            h_cps[sign * 4].wait_recv()
            blk = rows(hb, (x * NZ + lax.rem(z - sign * 4 + NZ, NZ)) * 16, 16)
            for s in (4, 3, 2, 1) if sign > 0 else (3, 2, 1):
                n = sign * (4 + s)
                h_cps[n] = send(blk, blk, hsend.at[n % NZ], hrecv.at[n % NZ], at_z(sign * s))
        for d in (4, -4):
            over_x(d)
        for d in (1, -1, 2, -2, 3, -3, 5, -5, 6, -6, 7, -7, 8):
            h_cps[d].wait_recv()
            over_x(d)
        for cp in f_cps:
            cp.wait_recv()

    with jax.named_scope("compact"):
        p, s = iota((4 * ZR, NZ * 16), 0), iota((4 * ZR, NZ * 16), 1)
        quarter = quotient(p, ZR)
        m = p - quarter * ZR
        who = quotient(m, R)
        pick = onehot(s == who * 16 + quarter * 4 + (m - who * R))
        for g in range(NX):
            got = mm(pick, hb[g * NZ * 16 : (g + 1) * NZ * 16, :]).astype(BF)
            for q in range(4):
                nm[g * ZR : (g + 1) * ZR, q * QW : (q + 1) * QW] = got[q * ZR : (q + 1) * ZR]
        p, s = iota((ZR, NZ * 16), 0), iota((ZR, NZ * 16), 1)
        who = quotient(p, R)
        pick = onehot(s == who * 16 + (p - who * R) * 4 + R)
        for g in range(NX):
            gu[g * ZR : (g + 1) * ZR, FC : FC + 16] = mm(
                pick, hb[g * NZ * 16 : (g + 1) * NZ * 16, 0:128]
            )[:, 0:16].astype(BF)

    with jax.named_scope("gate_up"):
        tokens = nm[...]
        y_cps = []
        for h in range(2):
            for lo, hi in ((0, 512), (512, FC)):
                gu[h * ROWS : (h + 1) * ROWS, lo:hi] = mm_t(tokens, wgu[h * FC + lo : h * FC + hi, :]).astype(BF)
            for d in range(1, NX):
                to = lax.rem(y + d, NX)
                n = h * 3 + d - 1
                y_cps.append(
                    send(
                        rows(gu, h * ROWS + to * ZR, ZR), rows(gr, h * ROWS + y * ZR, ZR),
                        gsend.at[n], grecv.at[n], at_y(d),
                    )
                )

    with jax.named_scope("activation"):
        b_cps = []
        for h in range(2):
            for cp in y_cps[h * 3 : h * 3 + 3]:
                cp.wait_recv()
            here = pl.ds(pl.multiple_of(h * ROWS + y * ZR, 16), ZR)
            gr[here, :] = gu[here, :]
            terms = [gr[h * ROWS + g * ZR : h * ROWS + (g + 1) * ZR, :].astype(F32) for g in range(NX)]
            if h == 0:
                for cp in g_cps:
                    cp.wait_recv()
                notes = [v[:, FC : FC + 16] for v in terms]
                means = [n[:, 8:9] for n in notes]
                sums = [n[:, 9:10] + n[:, 10:11] for n in notes]
                squares = [n[:, 11:12] + n[:, 12:13] for n in notes]
                center = sum(v + WD * m for v, m in zip(sums, means)) / D
                apart = [m - center for m in means]
                spread = sum(q + 2.0 * a * v + WD * a * a for q, a, v in zip(squares, apart, sums)) / D
                norm = lax.rsqrt(spread + EPS)
                lane = iota((ZR, 16), 1)
                share0 = jnp.sum(jnp.where(lane == x * 2, notes[0], 0.0), axis=1, keepdims=True)
                share1 = jnp.sum(jnp.where(lane == x * 2 + 1, notes[0], 0.0), axis=1, keepdims=True)
                share = jnp.where(iota((ZR, F2), 1) >= F2 // 2, share1, share0)
            whole = (terms[0] + terms[1])[:, :FC] + (terms[2] + terms[3])[:, :FC]
            for g in range(NX):
                whole = whole + apart[g] * gs[g * 8 : g * 8 + 1, :][:, h * FC : (h + 1) * FC]
            whole = whole * norm
            gate, up = whole[:, :F2], whole[:, F2:]
            ac[here, 0:F2] = (gate / (1.0 + jnp.exp(-gate)) * up * share).astype(BF)
            mine = rows(ac, h * ROWS + y * ZR, ZR)
            for d in range(1, NX):
                n = h * 3 + d - 1
                b_cps.append(send(mine, mine, bsend.at[n], brecv.at[n], at_y(d)))

    with jax.named_scope("activation_gather"):
        for cp in b_cps:
            cp.wait_recv()
        sends += y_cps + b_cps + g_cps

    with jax.named_scope("down"):
        act = [ac[h * ROWS : (h + 1) * ROWS, 0:F2] for h in range(2)]
        m_cps = []
        for t in range(NT):
            cols = slice(t * WT, (t + 1) * WT)
            for lo in range(0, WT, 512):
                ms[:, lo : lo + 512] = sum(
                    mm(act[h], wdn[h * F2 : (h + 1) * F2, lo : lo + 512]) for h in range(2)
                ).astype(BF)
            for d in range(1, NX):
                to = lax.rem(x + d, NX)
                n = t * 3 + d - 1
                m_cps.append(
                    send(
                        ms.at[pl.ds(pl.multiple_of(to * ZR, 16), ZR), cols],
                        mr.at[pl.ds(pl.multiple_of(x * ZR, 16), ZR), cols],
                        msend.at[n], mrecv.at[n], at_x(d),
                    )
                )

    p, s = iota((NZ * 16, ZR), 0), iota((NZ * 16, ZR), 1)
    wanted = (s == (p >> 4) * R + (p & 3)) & ((p & 3) < R)
    picks = [onehot(wanted & (((p >> 2) & 3) == q)) for q in range(4)]
    z_cps = {}

    def piece(t, d):
        return pl.ds(pl.multiple_of(t * NZ * 16 + lax.rem(z + d + NZ, NZ) * 16, 16), 16)

    def slot(t, n, k):
        return slice((t * n + k) * 16, (t * n + k + 1) * 16)

    def sum_over_x(t):
        cols = slice(t * WT, (t + 1) * WT)
        for cp in m_cps[t * 3 : t * 3 + 3]:
            cp.wait_recv()
        here = pl.ds(pl.multiple_of(x * ZR, 16), ZR)
        mr[here, cols] = ms[here, cols]
        total = mr[0:ZR, cols].astype(F32)
        for g in range(1, NX):
            total = total + mr[g * ZR : (g + 1) * ZR, cols].astype(F32)
        total = total.astype(BF)
        tiles = jnp.zeros((NZ * 16, WT // 4), F32)
        for q in range(4):
            tiles = tiles + mm(picks[q], total[:, q * WT // 4 : (q + 1) * WT // 4])
        zs[t * NZ * 16 : (t + 1) * NZ * 16, :] = tiles.astype(BF)
        for k, d in ((3, 8), (2, 7), (6, -7), (1, 6), (5, -6), (0, 5), (4, -5)):
            to = d - 4 if d > 0 else d + 4
            n = t * 15 + k
            z_cps[n] = send(zs.at[piece(t, d)], zl.at[slot(t, 7, k)], zsend.at[n], zrecv.at[n], at_z(to))
        for k, d in ((2, 3), (5, -3), (1, 2), (4, -2), (0, 1), (3, -1)):
            n = t * 15 + 7 + k
            z_cps[n] = send(zs.at[piece(t, d)], zr.at[slot(t, 8, k)], zsend.at[n], zrecv.at[n], at_z(d))

    def relay(t):
        for way, d, ks in ((0, 4, (0, 1, 2, 3)), (1, -4, (4, 5, 6))):
            total = zs[piece(t, d), :].astype(F32)
            for k in ks:
                z_cps[t * 15 + k].wait_recv()
                total = total + zl[slot(t, 7, k), :].astype(F32)
            zc[slot(t, 2, way), :] = total.astype(BF)
            n = t * 15 + 13 + way
            z_cps[n] = send(zc.at[slot(t, 2, way)], zr.at[slot(t, 8, 6 + way)], zsend.at[n], zrecv.at[n], at_z(d))

    with jax.named_scope("expert_sums"):
        sum_over_x(0)
        relay(0)
    with jax.named_scope("last_sum"):
        for t in range(NT):
            total = zs[piece(t, 0), :].astype(F32)
            for k in range(8):
                z_cps[t * 15 + 7 + k].wait_recv()
                total = total + zr[slot(t, 8, k), :].astype(F32)
            for q in range(4):
                out_ref[:, q * QW : (q + 1) * QW] = (hidden + total)[q * 4 : q * 4 + R].astype(BF)

    with jax.named_scope("drain"):
        for cp in a_cps + o_cps + c_cps + w_cps + m_cps + list(z_cps.values()) + list(h_cps.values()) + f_cps + sends:
            cp.wait_send()


def on_device(
    queries, new_key, new_value, cache_keys, cache_values, lengths, out_proj, residual, norm_gain,
    expert_ids, gate_weights, gate_proj, up_proj, down_proj,
):
    vmem = pl.BlockSpec(memory_space=pltpu.VMEM)
    dma = pltpu.SemaphoreType.DMA
    return pl.pallas_call(
        kernel,
        out_shape=jax.ShapeDtypeStruct((R, WD), BF),
        in_specs=[pl.BlockSpec(memory_space=pltpu.SMEM)] + [pl.BlockSpec(memory_space=pl.ANY)] * 13,
        out_specs=vmem,
        scratch_shapes=[
            pltpu.VMEM((R, KG), BF),
            pltpu.VMEM((R, HD), BF),
            pltpu.VMEM((R, HD), BF),
            pltpu.VMEM((R, SPAN, HD), BF),
            pltpu.VMEM((R, SPAN, HD), BF),
            pltpu.VMEM((KR, WD), BF),
            pltpu.VMEM((4 * R, WD), BF),
            pltpu.VMEM((WD,), BF),
            pltpu.VMEM((4, 4 * R), jnp.int32),
            pltpu.VMEM((4, 4 * R), BF),
            pltpu.VMEM((2 * FC, WD), BF),
            pltpu.VMEM((FC, WD), BF),
            pltpu.VMEM((16 * KR, WD // 2), BF),
            pltpu.VMEM((16 * 32, HD), BF),
            pltpu.VMEM((128, 16 * KR), BF),
            pltpu.VMEM((256, QW), BF),
            pltpu.VMEM((256, QW), BF),
            pltpu.VMEM((NX * 8, 2 * FC), F32),
            pltpu.VMEM((NX * NZ * 16, QW), BF),
            pltpu.VMEM((ROWS, WD), BF),
            pltpu.VMEM((2 * ROWS, GW), BF),
            pltpu.VMEM((2 * ROWS, GW), BF),
            pltpu.VMEM((2 * ROWS, 384), BF),
            pltpu.VMEM((ROWS, WD), BF),
            pltpu.VMEM((ROWS, WD), BF),
            pltpu.VMEM((NT * NZ * 16, WT // 4), BF),
            pltpu.VMEM((NT * 7 * 16, WT // 4), BF),
            pltpu.VMEM((NT * 2 * 16, WT // 4), BF),
            pltpu.VMEM((NT * 8 * 16, WT // 4), BF),
            dma((13,)),
            dma((3,)), dma((3,)),
            dma((6,)), dma((6,)),
            dma((4,)), dma((4,)),
            dma((16,)), dma((16,)),
            dma((16,)), dma((16,)),
            dma((3,)), dma((3,)),
            dma((NZ,)), dma((NZ,)),
            dma((3 * NZ,)), dma((3 * NZ,)),
            dma((6,)), dma((6,)),
            dma((6,)), dma((6,)),
            dma((3 * NT,)), dma((3 * NT,)),
            dma((15 * NT,)), dma((15 * NT,)),
        ],
        compiler_params=pltpu.CompilerParams(
            collective_id=0, has_side_effects=True, vmem_limit_bytes=62 << 20
        ),
        name="decode_layer",
    )(
        lengths, queries, new_key, new_value, cache_keys, cache_values,
        out_proj.reshape(KR, WD), residual, norm_gain, expert_ids.T, gate_weights.T,
        gate_proj.reshape(F2, WD), up_proj.reshape(F2, WD), down_proj.reshape(F2, WD),
    )


def solution(mesh):
    placed = (
        P(("attn", "eslice"), "egrp"),
        P(("attn", "eslice"), "egrp"),
        P(("attn", "eslice"), "egrp"),
        P(("attn", "eslice"), None, "egrp"),
        P(("attn", "eslice"), None, "egrp"),
        P(("attn", "eslice")),
        P("egrp", "attn", "eslice"),
        P("attn", "eslice"),
        P("eslice"),
        P("attn", None),
        P("attn", None),
        P("egrp", "attn", "eslice"),
        P("egrp", "attn", "eslice"),
        P("egrp", "attn", "eslice"),
    )
    return jax.shard_map(
        on_device, mesh=mesh, in_specs=placed, out_specs=P(("attn", "egrp"), "eslice"), check_vma=False
    )
```

```python
import functools
import math

import jax
import jax.numpy as jnp
from jax import lax
from jax.experimental import pallas as pl
from jax.experimental.pallas import tpu as pltpu
from jax.sharding import PartitionSpec as P

D = 6144
HD = 128
HG = 6
SPAN = 512
R = 3
EPS = 1e-05
NZ, NX = 16, 4
WD = D // NX
QW = WD // 4
KR = 24
KG = 768
F2 = 336
FC = 2 * F2
ZR = NZ * R
NT, WT = 1, WD
GW = 768
ROWS = NX * ZR
MESH = pl.DeviceIdType.MESH
BF = jnp.bfloat16
F32 = jnp.float32


def iota(shape, dim):
    return lax.broadcasted_iota(jnp.int32, shape, dim)


def onehot(cond):
    return jnp.where(cond, 1.0, 0.0).astype(BF)


def quotient(v, n):
    return (v * (65536 // n + 1)) >> 16


def mm(a, b):
    return jnp.dot(a, b, preferred_element_type=F32)


def mm_t(a, b):
    return lax.dot_general(a, b, (((1,), (1,)), ((), ())), preferred_element_type=F32)


def kernel(
    len_ref, q_hbm, nk_hbm, nv_hbm, ck_hbm, cv_hbm, op_hbm, res_hbm, gain_hbm, eid_hbm, gw_hbm,
    wg_ref, wu_ref, wd_ref,
    out_ref,
    qv, nkv, nvv, ckv, cvv, opv, resv, gainv, eidv, gwv, wgu, wdn, w2, at, a2, xs, xr, gs, hb, nm, gu, gr, ac, ms, mr, zs, zl, zc, zr,
    load_sem, wsend, wrecv, osend, orecv, csend, crecv, asend, arecv, xsend, xrecv, tsend, trecv,
    hsend, hrecv, fsend, frecv, gsend, grecv, bsend, brecv, msend, mrecv, zsend, zrecv,
):
    attn = lax.axis_index("attn")
    z, c = attn // 2, lax.rem(attn, 2)
    x, y = lax.axis_index("egrp"), lax.axis_index("eslice")

    def at_z(d):
        return (lax.rem(z + d + NZ, NZ) * 2 + c, x, y)

    def at_x(d):
        return (attn, lax.rem(x + d, NX), y)

    def at_y(d):
        return (attn, x, lax.rem(y + d, NX))

    quad, seat = z // 4, lax.rem(z, 4)

    def in_quad(s, dx, dy):
        return ((quad * 4 + s) * 2 + c, lax.rem(x + dx, NX), lax.rem(y + dy, NX))

    sibling = (z * 2 + 1 - c, x, y)
    others = [(k // 4, k % 4) for k in range(1, 16)]
    peers = [sibling]
    peers += [at_z(d) for d in range(-4, 5) if d]
    peers += [at_x(d) for d in range(1, NX)] + [at_y(d) for d in range(1, NX)]
    peers += [in_quad(lax.rem(seat + k, 4), m, 0) for k, m in others if k and m]
    peers += [in_quad(lax.rem(seat + k, 4), 0, m) for k, m in others if k and m]

    def send(src, dst, ssem, rsem, to):
        cp = pltpu.make_async_remote_copy(
            src_ref=src, dst_ref=dst, send_sem=ssem, recv_sem=rsem, device_id=to, device_id_type=MESH
        )
        cp.start()
        return cp

    def rows(ref, start, n):
        return ref.at[pl.ds(pl.multiple_of(start, 16), n)]

    barrier = pltpu.get_barrier_semaphore()
    for p in peers:
        pl.semaphore_signal(barrier, inc=1, device_id=p, device_id_type=MESH)

    def load(src, dst, sem):
        cp = pltpu.make_async_copy(src, dst, sem)
        cp.start()
        return cp

    l_q, l_nk, l_nv, l_ck, l_cv, l_op = [
        load(src, dst, load_sem.at[k])
        for k, (src, dst) in enumerate(
            ((q_hbm, qv), (nk_hbm, nkv), (nv_hbm, nvv), (ck_hbm, ckv), (cv_hbm, cvv), (op_hbm, opv))
        )
    ]
    l_rest = [
        load(src, dst, load_sem.at[k + 6])
        for k, (src, dst) in enumerate(((res_hbm, resv), (gain_hbm, gainv), (eid_hbm, eidv), (gw_hbm, gwv)))
    ]
    expert_weights = ((wg_ref, wgu, c * FC), (wu_ref, wgu, c * FC + F2), (wd_ref, wdn, c * F2))
    loads = [
        load(src, rows(dst, base, F2), load_sem.at[k + 10])
        for k, (src, dst, base) in enumerate(expert_weights)
    ]

    l_op.wait()
    own = opv[...].astype(F32)
    block = jnp.concatenate([own[:, : WD // 2], own[:, WD // 2 :]], axis=0).astype(BF)
    w2[pl.ds(pl.multiple_of((quad * 2 + c) * 2 * KR, 16), 2 * KR), :] = block

    sends = []
    with jax.named_scope("entry"):
        pl.semaphore_wait(barrier, len(peers))

    def block_of(d):
        return rows(w2, (lax.rem(quad - d + 8, 4) * 2 + c) * 2 * KR, 2 * KR)

    def pass_block(d, half, k, to):
        part = w2.at[
            pl.ds(pl.multiple_of((lax.rem(quad - d + 8, 4) * 2 + c) * 2 * KR, 16), 2 * KR), half * QW : (half + 1) * QW
        ]
        return send(part, part, osend.at[k], orecv.at[k], at_z(to))

    o_cps = [pass_block(0, 0, 0, 4), pass_block(0, 1, 1, -4), pass_block(0, 1, 2, 4), pass_block(0, 0, 3, -4)]
    c_cps = [send(block_of(0), block_of(0), csend.at[0], crecv.at[0], sibling)]

    with jax.named_scope("attention"):
        for cp in (l_q, l_nk, l_nv, l_ck, l_cv):
            cp.wait()
        qf = qv[...].astype(F32)
        pad2 = jnp.zeros((2, HD), F32)
        pieces = []
        for r in range(R):
            pieces += [qf[r : r + 1, h * HD : (h + 1) * HD] for h in range(HG)] + [pad2]
        q24 = jnp.concatenate(pieces, axis=0)
        q32 = jnp.concatenate([q24, jnp.zeros((8, HD), F32)], axis=0).astype(BF)
        nk24 = jnp.concatenate([jnp.broadcast_to(nkv[r : r + 1, :].astype(F32), (8, HD)) for r in range(R)], 0)
        nv24 = jnp.concatenate([jnp.broadcast_to(nvv[r : r + 1, :].astype(F32), (8, HD)) for r in range(R)], 0)
        len24 = jnp.concatenate([jnp.full((8, 1), len_ref[r], jnp.int32) for r in range(R)], 0)
        scale = 1.0 / math.sqrt(HD)
        scores = jnp.concatenate([mm_t(q32, ckv[r])[r * 8 : (r + 1) * 8] for r in range(R)], 0) * scale
        self_score = jnp.sum(q24 * nk24, axis=1, keepdims=True) * scale
        live = iota((R * 8, SPAN), 1) < len24
        scores = jnp.where(live, scores, -1e30)
        highest = jnp.maximum(jnp.max(scores, axis=1, keepdims=True), self_score)
        expos = jnp.where(live, jnp.exp(scores - highest), 0.0)
        own_exp = jnp.exp(self_score - highest)
        totals = jnp.sum(expos, axis=1, keepdims=True) + own_exp
        weights = jnp.concatenate([expos / totals, jnp.zeros((8, SPAN), F32)], axis=0).astype(BF)
        own_weight = (own_exp / totals).astype(BF).astype(F32)
        summed = jnp.concatenate([mm(weights, cvv[r])[r * 8 : (r + 1) * 8] for r in range(R)], 0)
        summed = summed + own_weight * nv24
        at[pl.ds(pl.multiple_of((seat * 4 + y) * 32, 16), 32), :] = jnp.concatenate(
            [summed, jnp.zeros((8, HD), F32)], axis=0
        ).astype(BF)

    mine = rows(at, (seat * 4 + y) * 32, 32)
    a_cps = [
        send(mine, mine, asend.at[k * 4 + m], arecv.at[k * 4 + m], in_quad(lax.rem(seat + k, 4), 0, m))
        for k, m in others
    ]
    w_cps = []
    for k, (src, dst, base) in enumerate(expert_weights):
        w_cps.append(send(src, rows(dst, base, F2), wsend.at[k], wrecv.at[k], sibling))

    for cp in l_rest:
        cp.wait()
    row16, lane16 = iota((16, 4 * R), 0), iota((16, 4 * R), 1)
    part = row16 & 3
    wanted = (lane16 == x * R + part) & (part < R)
    res16 = jnp.zeros((16, QW), F32)
    for q in range(4):
        res16 = res16 + mm(onehot(wanted & ((row16 >> 2) == q)), resv[:, q * QW : (q + 1) * QW])
    gain_row = gainv[...].reshape(1, WD)
    gain16 = jnp.concatenate(
        [jnp.broadcast_to(gain_row[:, q * QW : (q + 1) * QW].astype(F32), (4, QW)) for q in range(4)], 0
    )
    gwf = gwv[...].astype(F32)
    expert = iota((128, 4 * R), 0)
    shares = jnp.zeros((128, 4 * R), F32)
    for k in range(4):
        shares = shares + jnp.where(expert == eidv[k : k + 1, :], gwf[k : k + 1, :], 0.0)
    share16 = mm_t(onehot(lane16 == x * R + (row16 >> 2)), shares.astype(BF))

    with jax.named_scope("projection_relay"):
        o_cps[0].wait_recv()
        o_cps.append(pass_block(1, 0, 4, 4))
        o_cps[1].wait_recv()
        o_cps.append(pass_block(-1, 1, 5, -4))

    with jax.named_scope("attended_gather"):
        for cp in a_cps:
            cp.wait_recv()
        p, s = iota((HG * 64, 512), 0), iota((HG * 64, 512), 1)
        pick = onehot(s == ((p & 63) >> 2) * 32 + (p & 3) * 8 + (p >> 6))
        heads = mm(pick, at[...]).astype(BF)
        a64 = jnp.concatenate([heads[h * 64 : (h + 1) * 64] for h in range(HG)], axis=1)
        j = iota((1, 16 * KR), 1)
        slot = quotient(j, 2 * KR)
        rem = j - slot * 2 * KR
        later = rem >= KR
        source = (((slot >> 1) * 4 + seat) * 2 + (slot & 1)) * KR + jnp.where(later, rem - KR, rem)
        wide = mm(a64, onehot(iota((KG, 16 * KR), 0) == source))
        a2[...] = jnp.concatenate([jnp.where(later, 0.0, wide), jnp.where(later, wide, 0.0)], axis=0).astype(BF)

    with jax.named_scope("projection_gather"):
        for d, k in ((1, 2), (-1, 3)):
            o_cps[k].wait_recv()
            c_cps.append(send(block_of(d), block_of(d), csend.at[d % 4], crecv.at[d % 4], sibling))

    with jax.named_scope("gain_sums"):
        for cp in loads:
            cp.wait()
        for cp in w_cps:
            cp.wait_recv()
        gains = jnp.broadcast_to(gain_row, (16, WD))
        for lo, hi in ((0, 512), (512, 1024), (1024, 2 * FC)):
            gs[pl.ds(pl.multiple_of(y * 8, 8), 8), lo:hi] = mm_t(gains, wgu[lo:hi, :])[0:8]
        mine = gs.at[pl.ds(pl.multiple_of(y * 8, 8), 8)]
        g_cps = [send(mine, mine, tsend.at[d - 1], trecv.at[d - 1], at_y(d)) for d in range(1, NX)]

    with jax.named_scope("last_block"):
        o_cps[4].wait_recv()
        o_cps[5].wait_recv()
        c_cps.append(send(block_of(2), block_of(2), csend.at[2], crecv.at[2], sibling))

    with jax.named_scope("projection"):
        for cp in c_cps:
            cp.wait_recv()
        mixed = mm(a2[...], w2[...]).astype(BF)
        p, s = iota((256, 128), 0), iota((256, 128), 1)
        source = (((p >> 3) & 1) << 6) + ((p >> 4) << 2) + (p & 3)
        odd = ((p >> 2) & 1) == 1
        xs[...] = (
            mm(onehot((s == source) & ~odd), mixed[:, :QW]) + mm(onehot((s == source) & odd), mixed[:, QW:])
        ).astype(BF)

    with jax.named_scope("projection_terms"):
        slot = (seat * 4 + x) * 16
        cps = []
        for k, m in others:
            to = lax.rem(seat + k, 4)
            n = k * 4 + m
            cps.append(
                send(
                    rows(xs, (to * 4 + lax.rem(x + m, NX)) * 16, 16), rows(xr, slot, 16),
                    xsend.at[n], xrecv.at[n], in_quad(to, m, 0),
                )
            )
        for cp in cps:
            cp.wait_recv()
        sends += cps
        xr[pl.ds(pl.multiple_of(slot, 16), 16), :] = xs[pl.ds(pl.multiple_of(slot, 16), 16), :]
        hidden = res16
        for g in range(16):
            hidden = hidden + xr[g * 16 : (g + 1) * 16, :].astype(F32)
        hidden = hidden.astype(BF).astype(F32)

    with jax.named_scope("center_slice"):
        def per_request(v):
            v = jnp.sum(v, axis=1, keepdims=True)
            v = v[0:8] + v[8:16]
            v = v[0:4] + v[4:8]
            return jnp.concatenate([v] * 4, axis=0)

        def halves(v):
            high = v.astype(BF).astype(F32)
            return high, v - high

        mean = (per_request(hidden) / WD).astype(BF).astype(F32)
        inside = (iota((16, QW), 0) & 3) < R
        near = jnp.where(inside, hidden - mean, 0.0)
        notes = (mean,) + halves(per_request(near)) + halves(per_request(near * near))
        lane = iota((16, 128), 1)
        row = iota((16, 128), 0)
        extra = jnp.where(lane < 8, share16, 0.0)
        for j, note in enumerate(notes):
            by_request = jnp.concatenate([jnp.broadcast_to(note[i : i + 1], (4, 1)) for i in range(4)], axis=0)
            extra = extra + jnp.where(lane == 8 + j, by_request, 0.0)
        extra = jnp.where((row & 3) == R, extra, 0.0)
        extra = jnp.concatenate([extra, jnp.zeros((16, QW - 128), F32)], axis=1)
        hb[pl.ds(pl.multiple_of((x * NZ + z) * 16, 16), 16), :] = (near * gain16 + extra).astype(BF)

    with jax.named_scope("token_gather"):
        f_cps = []

        def over_x(d):
            blk = rows(hb, (x * NZ + lax.rem(z - d + NZ, NZ)) * 16, 16)
            for k in (2, 1, 3):
                n = (k - 1) * NZ + d % NZ
                f_cps.append(send(blk, blk, fsend.at[n], frecv.at[n], at_x(k)))

        blk = rows(hb, (x * NZ + z) * 16, 16)
        h_cps = {}
        for d in (4, -4, 3, -3, 2, -2, 1, -1):
            h_cps[d] = send(blk, blk, hsend.at[d % NZ], hrecv.at[d % NZ], at_z(d))
        over_x(0)
        for sign in (1, -1):
            h_cps[sign * 4].wait_recv()
            blk = rows(hb, (x * NZ + lax.rem(z - sign * 4 + NZ, NZ)) * 16, 16)
            for s in (4, 3, 2, 1) if sign > 0 else (3, 2, 1):
                n = sign * (4 + s)
                h_cps[n] = send(blk, blk, hsend.at[n % NZ], hrecv.at[n % NZ], at_z(sign * s))
        for d in (4, -4):
            over_x(d)
        for d in (1, -1, 2, -2, 3, -3, 5, -5, 6, -6, 7, -7, 8):
            h_cps[d].wait_recv()
            over_x(d)
        for cp in f_cps:
            cp.wait_recv()

    with jax.named_scope("compact"):
        p, s = iota((4 * ZR, NZ * 16), 0), iota((4 * ZR, NZ * 16), 1)
        quarter = quotient(p, ZR)
        m = p - quarter * ZR
        who = quotient(m, R)
        pick = onehot(s == who * 16 + quarter * 4 + (m - who * R))
        for g in range(NX):
            got = mm(pick, hb[g * NZ * 16 : (g + 1) * NZ * 16, :]).astype(BF)
            for q in range(4):
                nm[g * ZR : (g + 1) * ZR, q * QW : (q + 1) * QW] = got[q * ZR : (q + 1) * ZR]
        p, s = iota((ZR, NZ * 16), 0), iota((ZR, NZ * 16), 1)
        who = quotient(p, R)
        pick = onehot(s == who * 16 + (p - who * R) * 4 + R)
        for g in range(NX):
            gu[g * ZR : (g + 1) * ZR, FC : FC + 16] = mm(
                pick, hb[g * NZ * 16 : (g + 1) * NZ * 16, 0:128]
            )[:, 0:16].astype(BF)

    with jax.named_scope("gate_up"):
        tokens = nm[...]
        y_cps = []
        for h in range(2):
            for lo, hi in ((0, 512), (512, FC)):
                gu[h * ROWS : (h + 1) * ROWS, lo:hi] = mm_t(tokens, wgu[h * FC + lo : h * FC + hi, :]).astype(BF)
            for d in range(1, NX):
                to = lax.rem(y + d, NX)
                n = h * 3 + d - 1
                y_cps.append(
                    send(
                        rows(gu, h * ROWS + to * ZR, ZR), rows(gr, h * ROWS + y * ZR, ZR),
                        gsend.at[n], grecv.at[n], at_y(d),
                    )
                )

    with jax.named_scope("activation"):
        b_cps = []
        for h in range(2):
            for cp in y_cps[h * 3 : h * 3 + 3]:
                cp.wait_recv()
            here = pl.ds(pl.multiple_of(h * ROWS + y * ZR, 16), ZR)
            gr[here, :] = gu[here, :]
            terms = [gr[h * ROWS + g * ZR : h * ROWS + (g + 1) * ZR, :].astype(F32) for g in range(NX)]
            if h == 0:
                for cp in g_cps:
                    cp.wait_recv()
                notes = [v[:, FC : FC + 16] for v in terms]
                means = [n[:, 8:9] for n in notes]
                sums = [n[:, 9:10] + n[:, 10:11] for n in notes]
                squares = [n[:, 11:12] + n[:, 12:13] for n in notes]
                center = sum(v + WD * m for v, m in zip(sums, means)) / D
                apart = [m - center for m in means]
                spread = sum(q + 2.0 * a * v + WD * a * a for q, a, v in zip(squares, apart, sums)) / D
                norm = lax.rsqrt(spread + EPS)
                lane = iota((ZR, 16), 1)
                share0 = jnp.sum(jnp.where(lane == x * 2, notes[0], 0.0), axis=1, keepdims=True)
                share1 = jnp.sum(jnp.where(lane == x * 2 + 1, notes[0], 0.0), axis=1, keepdims=True)
                share = jnp.where(iota((ZR, F2), 1) >= F2 // 2, share1, share0)
            whole = (terms[0] + terms[1])[:, :FC] + (terms[2] + terms[3])[:, :FC]
            for g in range(NX):
                whole = whole + apart[g] * gs[g * 8 : g * 8 + 1, :][:, h * FC : (h + 1) * FC]
            whole = whole * norm
            gate, up = whole[:, :F2], whole[:, F2:]
            ac[here, 0:F2] = (gate / (1.0 + jnp.exp(-gate)) * up * share).astype(BF)
            mine = rows(ac, h * ROWS + y * ZR, ZR)
            for d in range(1, NX):
                n = h * 3 + d - 1
                b_cps.append(send(mine, mine, bsend.at[n], brecv.at[n], at_y(d)))

    with jax.named_scope("activation_gather"):
        for cp in b_cps:
            cp.wait_recv()
        sends += y_cps + b_cps + g_cps

    with jax.named_scope("down"):
        act = [ac[h * ROWS : (h + 1) * ROWS, 0:F2] for h in range(2)]
        m_cps = []
        for t in range(NT):
            cols = slice(t * WT, (t + 1) * WT)
            for lo in range(0, WT, 512):
                ms[:, lo : lo + 512] = sum(
                    mm(act[h], wdn[h * F2 : (h + 1) * F2, lo : lo + 512]) for h in range(2)
                ).astype(BF)
            for d in range(1, NX):
                to = lax.rem(x + d, NX)
                n = t * 3 + d - 1
                m_cps.append(
                    send(
                        ms.at[pl.ds(pl.multiple_of(to * ZR, 16), ZR), cols],
                        mr.at[pl.ds(pl.multiple_of(x * ZR, 16), ZR), cols],
                        msend.at[n], mrecv.at[n], at_x(d),
                    )
                )

    p, s = iota((NZ * 16, ZR), 0), iota((NZ * 16, ZR), 1)
    wanted = (s == (p >> 4) * R + (p & 3)) & ((p & 3) < R)
    picks = [onehot(wanted & (((p >> 2) & 3) == q)) for q in range(4)]
    z_cps = {}

    def piece(t, d):
        return pl.ds(pl.multiple_of(t * NZ * 16 + lax.rem(z + d + NZ, NZ) * 16, 16), 16)

    def slot(t, n, k):
        return slice((t * n + k) * 16, (t * n + k + 1) * 16)

    def sum_over_x(t):
        cols = slice(t * WT, (t + 1) * WT)
        for cp in m_cps[t * 3 : t * 3 + 3]:
            cp.wait_recv()
        here = pl.ds(pl.multiple_of(x * ZR, 16), ZR)
        mr[here, cols] = ms[here, cols]
        total = mr[0:ZR, cols].astype(F32)
        for g in range(1, NX):
            total = total + mr[g * ZR : (g + 1) * ZR, cols].astype(F32)
        total = total.astype(BF)
        tiles = jnp.zeros((NZ * 16, WT // 4), F32)
        for q in range(4):
            tiles = tiles + mm(picks[q], total[:, q * WT // 4 : (q + 1) * WT // 4])
        zs[t * NZ * 16 : (t + 1) * NZ * 16, :] = tiles.astype(BF)
        for k, d in ((3, 8), (2, 7), (6, -7), (1, 6), (5, -6), (0, 5), (4, -5)):
            to = d - 4 if d > 0 else d + 4
            n = t * 15 + k
            z_cps[n] = send(zs.at[piece(t, d)], zl.at[slot(t, 7, k)], zsend.at[n], zrecv.at[n], at_z(to))
        for k, d in ((2, 3), (5, -3), (1, 2), (4, -2), (0, 1), (3, -1)):
            n = t * 15 + 7 + k
            z_cps[n] = send(zs.at[piece(t, d)], zr.at[slot(t, 8, k)], zsend.at[n], zrecv.at[n], at_z(d))

    def relay(t):
        for way, d, ks in ((0, 4, (0, 1, 2, 3)), (1, -4, (4, 5, 6))):
            total = zs[piece(t, d), :].astype(F32)
            for k in ks:
                z_cps[t * 15 + k].wait_recv()
                total = total + zl[slot(t, 7, k), :].astype(F32)
            zc[slot(t, 2, way), :] = total.astype(BF)
            n = t * 15 + 13 + way
            z_cps[n] = send(zc.at[slot(t, 2, way)], zr.at[slot(t, 8, 6 + way)], zsend.at[n], zrecv.at[n], at_z(d))

    with jax.named_scope("expert_sums"):
        sum_over_x(0)
        relay(0)
    with jax.named_scope("last_sum"):
        for t in range(NT):
            total = zs[piece(t, 0), :].astype(F32)
            for k in range(8):
                z_cps[t * 15 + 7 + k].wait_recv()
                total = total + zr[slot(t, 8, k), :].astype(F32)
            for q in range(4):
                out_ref[:, q * QW : (q + 1) * QW] = (hidden + total)[q * 4 : q * 4 + R].astype(BF)

    with jax.named_scope("drain"):
        for cp in a_cps + o_cps + c_cps + w_cps + m_cps + list(z_cps.values()) + list(h_cps.values()) + f_cps + sends:
            cp.wait_send()


def on_device(
    queries, new_key, new_value, cache_keys, cache_values, lengths, out_proj, residual, norm_gain,
    expert_ids, gate_weights, gate_proj, up_proj, down_proj,
):
    vmem = pl.BlockSpec(memory_space=pltpu.VMEM)
    dma = pltpu.SemaphoreType.DMA
    return pl.pallas_call(
        kernel,
        out_shape=jax.ShapeDtypeStruct((R, WD), BF),
        in_specs=[pl.BlockSpec(memory_space=pltpu.SMEM)] + [pl.BlockSpec(memory_space=pl.ANY)] * 13,
        out_specs=vmem,
        scratch_shapes=[
            pltpu.VMEM((R, KG), BF),
            pltpu.VMEM((R, HD), BF),
            pltpu.VMEM((R, HD), BF),
            pltpu.VMEM((R, SPAN, HD), BF),
            pltpu.VMEM((R, SPAN, HD), BF),
            pltpu.VMEM((KR, WD), BF),
            pltpu.VMEM((4 * R, WD), BF),
            pltpu.VMEM((WD,), BF),
            pltpu.VMEM((4, 4 * R), jnp.int32),
            pltpu.VMEM((4, 4 * R), BF),
            pltpu.VMEM((2 * FC, WD), BF),
            pltpu.VMEM((FC, WD), BF),
            pltpu.VMEM((16 * KR, WD // 2), BF),
            pltpu.VMEM((16 * 32, HD), BF),
            pltpu.VMEM((128, 16 * KR), BF),
            pltpu.VMEM((256, QW), BF),
            pltpu.VMEM((256, QW), BF),
            pltpu.VMEM((NX * 8, 2 * FC), F32),
            pltpu.VMEM((NX * NZ * 16, QW), BF),
            pltpu.VMEM((ROWS, WD), BF),
            pltpu.VMEM((2 * ROWS, GW), BF),
            pltpu.VMEM((2 * ROWS, GW), BF),
            pltpu.VMEM((2 * ROWS, 384), BF),
            pltpu.VMEM((ROWS, WD), BF),
            pltpu.VMEM((ROWS, WD), BF),
            pltpu.VMEM((NT * NZ * 16, WT // 4), BF),
            pltpu.VMEM((NT * 7 * 16, WT // 4), BF),
            pltpu.VMEM((NT * 2 * 16, WT // 4), BF),
            pltpu.VMEM((NT * 8 * 16, WT // 4), BF),
            dma((13,)),
            dma((3,)), dma((3,)),
            dma((6,)), dma((6,)),
            dma((4,)), dma((4,)),
            dma((16,)), dma((16,)),
            dma((16,)), dma((16,)),
            dma((3,)), dma((3,)),
            dma((NZ,)), dma((NZ,)),
            dma((3 * NZ,)), dma((3 * NZ,)),
            dma((6,)), dma((6,)),
            dma((6,)), dma((6,)),
            dma((3 * NT,)), dma((3 * NT,)),
            dma((15 * NT,)), dma((15 * NT,)),
        ],
        compiler_params=pltpu.CompilerParams(
            collective_id=0, has_side_effects=True, vmem_limit_bytes=62 << 20
        ),
        name="decode_layer",
    )(
        lengths, queries, new_key, new_value, cache_keys, cache_values,
        out_proj.reshape(KR, WD), residual, norm_gain, expert_ids.T, gate_weights.T,
        gate_proj.reshape(F2, WD), up_proj.reshape(F2, WD), down_proj.reshape(F2, WD),
    )


def solution(mesh):
    placed = (
        P(("attn", "eslice"), "egrp"),
        P(("attn", "eslice"), "egrp"),
        P(("attn", "eslice"), "egrp"),
        P(("attn", "eslice"), None, "egrp"),
        P(("attn", "eslice"), None, "egrp"),
        P(("attn", "eslice")),
        P("egrp", "attn", "eslice"),
        P("attn", "eslice"),
        P("eslice"),
        P("attn", None),
        P("attn", None),
        P("egrp", "attn", "eslice"),
        P("egrp", "attn", "eslice"),
        P("egrp", "attn", "eslice"),
    )
    return jax.shard_map(
        on_device, mesh=mesh, in_specs=placed, out_specs=P(("attn", "egrp"), "eslice"), check_vma=False
    )
```
